32 devices in a mesh: groups: 2 (over y), ex: 4 (over z), layer: 4 (over x, core).
Axes of the slice: x: 2, y: 2, z: 4, core: 2. Of those that a mesh axis runs over, the one named last changes fastest.
Arguments:
- layer_inputs: bfloat16 [4, 1024, 1280], P('layer', ('groups', 'ex')), parts along dimension 1, may hold values from -6 to 6
- out_grads: bfloat16 [4, 1024, 5120], P('layer', ('groups', 'ex')), parts along dimension 1, may hold values from -6 to 6
- proj_in: bfloat16 [4, 1280, 32], P('layer'), may hold values from -0.15625 to 0.15625
- proj_out: bfloat16 [4, 5120, 32], P('layer'), may hold values from -0.078125 to 0.078125
- frame_lengths: int32 [8, 16], P(('groups', 'ex')), parts along dimension 0, may hold values from 1 to 32, 128 in all within a row
- query_ids: int32 [512], P('groups'), parts along dimension 0, may hold values from 0 to 63
Outputs:
- scores: float32 [512, 64], P('groups', 'ex'), parts along dimension 0
The draws below stay inside these ranges and needn't reach their ends.
There are 2 independent parts, one for each index of `groups`. The reference program is written for one: setup_inputs(seed, part) draws one part's arguments, and reference() takes and returns one part's arrays. A program takes and returns all parts, laid end to end along the dimension named above; an argument that names none is the same for every part. Nothing has to cross between parts.
Inputs may be any that keep to these rules, and one draw needn't show every extreme that they name: `frame_lengths`: each row fills the 128 frames of one index of ex.
All inputs are finite; a program needn't handle non-finite values.
Results may differ from the reference program's by a relative error of at most 0.0003.
Values sent between devices are 32-bit elements; how exact they have to be, the bound alone decides.
No kernel may reach another device: no remote copies, remote signals or barrier semaphores. Data moves between devices by JAX's collectives and lax.ppermute only.
A program may use at most 64 MiB of HBM per device.

```python
import math
import jax
import jax.numpy as jnp
import numpy as np
from jax import lax

D = 1280
FF = 5120
R = 32
K = 1024
FRAMES_DEV = 128
EX_DEV = 16
Q = 256
MOST = 32
EX_GROUPS = 4
EXAMPLES = 64
FRAMES = 512
LAYERS = 4


def touch_ends(drawn, stream_key, low, high):
    place = [jax.random.randint(jax.random.fold_in(stream_key, axis), (), 0, length) for axis, length in enumerate(drawn.shape)]
    widest = drawn.shape.index(max(drawn.shape))
    neighbour = place[:widest] + [(place[widest] + 1) % drawn.shape[widest]] + place[widest + 1:]
    return drawn.at[tuple(place)].set(low).at[tuple(neighbour)].set(high)


def steps_of(key, dims, cuts, least, high):
    loudness = 1.0
    for dim, shards_of in cuts:
        draws = jax.random.uniform(jax.random.fold_in(jax.random.fold_in(key, 6), dim), (shards_of,), jnp.float32, least / len(cuts), high / len(cuts))
        loudness = loudness * jnp.repeat(jnp.exp(draws), dims[dim] // shards_of).reshape((-1,) + (1,) * (len(dims) - 1 - dim))
    return loudness


def split_up(number_of, total, bound, slope):
    weights = [(1 << 20) // math.isqrt(grade ** slope) + 1 for grade in range(2, number_of + 1)]
    spare, holding = total - bound - (number_of - 1), [1] * (number_of - 1)
    while spare > 0:
        movable = [i for i in range(number_of - 1) if holding[i] < bound]
        pool, left = sum([weights[i] for i in movable]), spare
        for i in movable:
            extra = min(bound - holding[i], max(1, left * weights[i] // pool), spare)
            holding[i] = holding[i] + extra
            spare = spare - extra
    return np.array([bound] + holding)


def ragged(own_key, number_of, total, bound, skew):
    if number_of == 2:
        one = jax.random.randint(own_key, (), max(1, total - bound), min(bound, total - 1) + 1)
        return jnp.stack([one, total - one])
    lengths = jnp.asarray(split_up(number_of, total, bound, skew), jnp.int32)
    twos = (number_of - 1) // 2
    donor, taker = lengths[1:1 + 2 * twos:2], lengths[2:2 + 2 * twos:2]
    room = jnp.minimum(donor - 1, bound - taker)
    passed = jax.random.randint(jax.random.fold_in(own_key, 1), (twos,), 0, 1 << 20) % (room + 1)
    lengths = lengths.at[1:1 + 2 * twos:2].set(donor - passed).at[2:2 + 2 * twos:2].set(taker + passed)
    return lengths[jax.random.permutation(jax.random.fold_in(own_key, 2), number_of)]


def scatter_about(key, dims, spread, reach, split=(), held_as=jnp.bfloat16):
    level = steps_of(key, dims, split, -0.22, 0.18) if split else 1.0
    entries = jax.random.normal(key, dims, jnp.float32) * spread * level
    return jnp.minimum(jnp.maximum(entries, -reach), reach).astype(held_as)


def setup_inputs(seed: int = 0, part: int = 0) -> dict:
    key_list = jax.random.split(jax.random.key(seed), 7)
    own_keys = jax.random.split(jax.random.fold_in(key_list[6], part), 7)
    return {
        "layer_inputs": scatter_about(own_keys[0], (LAYERS, FRAMES, D), 1.0, 6.0, ((0, 4), (1, 4))),
        "out_grads": scatter_about(own_keys[1], (LAYERS, FRAMES, FF), 1.0, 6.0, ((0, 4), (1, 4))),
        "proj_in": scatter_about(key_list[2], (LAYERS, D, R), D ** -0.5, 0.15625, ((0, 4),)),
        "proj_out": scatter_about(key_list[3], (LAYERS, FF, R), FF ** -0.5, 0.078125, ((0, 4),)),
        "frame_lengths": jax.vmap(lambda own: ragged(own, EX_DEV, FRAMES_DEV, MOST, 2))(jax.random.split(own_keys[4], EX_GROUPS)).reshape((EX_GROUPS, EX_DEV)).astype(jnp.int32),
        "query_ids": touch_ends(jax.random.randint(own_keys[5], (Q,), 0, EXAMPLES), jax.random.fold_in(own_keys[5], 1), 0, EXAMPLES - 1).astype(jnp.int32),
    }


def reference(layer_inputs, out_grads, proj_in, proj_out, frame_lengths, query_ids):
    end_frames = jnp.cumsum(frame_lengths, axis=1)
    starts = end_frames - frame_lengths
    positions = jnp.arange(FRAMES_DEV, dtype=jnp.int32)
    member = ((positions[None, None, :] >= starts[:, :, None]) & (positions[None, None, :] < end_frames[:, :, None])).astype(jnp.float32)
    example_ids = jnp.arange(EXAMPLES, dtype=jnp.int32)
    chosen = (query_ids[:, None] == example_ids[None, :]).astype(jnp.float32)
    score_total = jnp.zeros((Q, EXAMPLES), jnp.float32)
    for layer_idx in range(LAYERS):
        in_proj = jnp.dot(layer_inputs[layer_idx].astype(jnp.float32), proj_in[layer_idx].astype(jnp.float32), preferred_element_type=jnp.float32)
        out_proj = jnp.dot(out_grads[layer_idx].astype(jnp.float32), proj_out[layer_idx].astype(jnp.float32), preferred_element_type=jnp.float32)
        outer_terms = (out_proj[:, :, None] * in_proj[:, None, :]).reshape(EX_GROUPS, FRAMES_DEV, K)
        features = jnp.einsum('nef,nfk->nek', member, outer_terms, precision=lax.Precision.HIGHEST).reshape(EXAMPLES, K)
        gram_matrix = jnp.dot(features.T, features, precision=lax.Precision.HIGHEST)
        damping = 0.1 * jnp.trace(gram_matrix) / K
        factor = jnp.linalg.cholesky(gram_matrix + damping * jnp.eye(K, dtype=jnp.float32))
        queries = jnp.dot(chosen, features, precision=lax.Precision.HIGHEST)
        precond = jax.scipy.linalg.cho_solve((factor, True), queries.T).T
        score_total = score_total + jnp.dot(precond, features.T, precision=lax.Precision.HIGHEST)
    return score_total
```

```python
import functools

import jax
import jax.numpy as jnp
from jax import lax
from jax.experimental import pallas as pl
from jax.experimental.pallas import tpu as pltpu
from jax.sharding import PartitionSpec as P

F32 = jnp.float32
BF16 = jnp.bfloat16
CHUNKS = 4


def nt(a, b):
    return lax.dot_general(a, b, (((1,), (1,)), ((), ())), preferred_element_type=F32)


def nn(a, b):
    return lax.dot_general(a, b, (((1,), (0,)), ((), ())), preferred_element_type=F32)


def tn(a, b):
    return lax.dot_general(a, b, (((0,), (0,)), ((), ())), preferred_element_type=F32)


def split3(x):
    hi = x.astype(BF16)
    rest = x - hi.astype(F32)
    mid = rest.astype(BF16)
    low = (rest - mid.astype(F32)).astype(BF16)
    return hi, mid, low


def split2(x):
    hi = x.astype(BF16)
    return hi, (x - hi.astype(F32)).astype(BF16)


def mm(a, b):
    ah, al = split2(a)
    bh, bl = split2(b)
    return nn(ah, bh) + (nn(ah, bl) + nn(al, bh))


def exact_nn(a, b):
    return lax.dot_general(a, b, (((1,), (0,)), ((), ())), precision=lax.Precision.HIGHEST, preferred_element_type=F32)


def project_kernel(lens_hbm, li_ref, og_ref, pi_ref, po_ref, out_ref, lens_ref, li_v, og_v, pi_v, po_v, sems):
    ff = og_ref.shape[2]
    step = ff // CHUNKS
    copies = [
        pltpu.make_async_copy(pi_ref.at[0], pi_v, sems.at[0]),
        pltpu.make_async_copy(li_ref.at[0], li_v, sems.at[1]),
        pltpu.make_async_copy(po_ref.at[0], po_v, sems.at[2]),
        pltpu.make_async_copy(lens_hbm, lens_ref, sems.at[3]),
    ]
    for c in range(CHUNKS):
        cols = pl.ds(c * step, step)
        copies.append(pltpu.make_async_copy(og_ref.at[0, :, cols], og_v.at[:, cols], sems.at[4 + c]))
    for copy in copies:
        copy.start()
    rank = pi_ref.shape[1]
    frames = li_ref.shape[1]
    positions = lax.broadcasted_iota(jnp.int32, (8, frames), 1)
    copies[3].wait()
    ids = jnp.zeros((8, frames), F32)
    end = lens_ref[0, 0]
    for j in range(1, lens_ref.shape[1]):
        ids = ids + jnp.where(positions >= end, 1.0, 0.0)
        end = end + lens_ref[0, j]
    out_ref[2 * rank:, :] = ids
    copies[0].wait()
    copies[1].wait()
    out_ref[rank:2 * rank, :] = nt(pi_v[...], li_v[...])
    copies[2].wait()
    total = jnp.zeros((rank, frames), F32)
    for c in range(CHUNKS):
        copies[4 + c].wait()
        total = total + nt(po_v[:, c * step:(c + 1) * step], og_v[:, c * step:(c + 1) * step])
    out_ref[:rank, :] = total


def solve_kernel(width, per_dev, rank, *refs):
    packets, out_ref, s_ref = refs[:-2], refs[-2], refs[-1]
    frames = packets[0].shape[1]
    count = len(packets)
    total = count * per_dev

    def terms(lo):
        x = jnp.concatenate([p[lo:lo + rank, :] for p in packets], axis=1)
        hi, mid, low = split3(x)
        return (
            jnp.concatenate([hi, hi, mid, hi, low, mid], axis=0),
            jnp.concatenate([hi, mid, hi, low, hi, mid], axis=0),
        )

    left_o, right_o = terms(0)
    left_i, right_i = terms(rank)
    row = lax.broadcasted_iota(jnp.int32, (total, frames), 0).astype(F32)
    member = jnp.concatenate(
        [jnp.where(p[2 * rank:2 * rank + 1, :] + float(k * per_dev) == row, 1.0, 0.0) for k, p in enumerate(packets)], axis=1
    ).astype(BF16)
    kernel = jnp.zeros((total, total), F32)
    for k in range(count):
        cols = slice(k * frames, (k + 1) * frames)
        block = tn(left_o[:, cols], right_o) * tn(left_i[:, cols], right_i)
        hi, mid, low = split3(block)
        part = (nt(low, member) + nt(mid, member)) + nt(hi, member)
        hi, mid, low = split3(part)
        m = member[:, cols]
        kernel = kernel + ((nn(m, low) + nn(m, mid)) + nn(m, hi))

    ids0 = lax.broadcasted_iota(jnp.int32, (total, total), 0)
    ids1 = lax.broadcasted_iota(jnp.int32, (total, total), 1)
    diagonal = ids0 == ids1
    eye = jnp.where(diagonal, 1.0, 0.0)
    damp = jnp.sum(jnp.where(diagonal, kernel, 0.0), keepdims=True) * (0.1 / width)
    scale = jnp.sum(jnp.where(diagonal, kernel, 0.0), axis=0, keepdims=True) + damp
    ratio = damp / scale
    column = jnp.sum(jnp.where(diagonal, ratio, 0.0), axis=1, keepdims=True)
    e1 = jnp.where(diagonal, 0.0, -kernel / scale)
    mine = e1[:per_dev] + eye[:per_dev]
    e2 = mm(e1, e1)
    mine = mine + mm(mine, e2)
    e4 = mm(e2, e2)
    mine = mine + mm(mine, e4)
    e8 = mm(e4, e4)
    mine = mine + mm(mine, e8)
    squares = e8 * e8
    left = jnp.sum(squares * column)
    spread = jnp.sum(squares * column * (scale / damp))
    good = (left <= 1e-5) & (spread <= 0.02)
    s_ref[...] = eye[:per_dev] - column[:per_dev] * mine

    @pl.when(jnp.logical_not(good))
    def _():
        full = kernel + damp * eye

        def sweep(k, a):
            r = jnp.sum(jnp.where(ids0 == k, a, 0.0), axis=0, keepdims=True)
            c = jnp.sum(jnp.where(ids1 == k, a, 0.0), axis=1, keepdims=True)
            p = 1.0 / jnp.sum(jnp.where(ids1[:1] == k, r, 0.0), axis=1, keepdims=True)
            inner = a - c * (r * p)
            edge = jnp.where(ids0 == k, r * p, c * p)
            swept = jnp.where((ids0 == k) | (ids1 == k), edge, inner)
            return jnp.where((ids0 == k) & (ids1 == k), -p, swept)

        inverse = -lax.fori_loop(0, total, sweep, full)
        inverse = inverse + exact_nn(inverse, eye - exact_nn(full, inverse))
        s_ref[...] = eye[:per_dev] - damp * inverse[:per_dev]

    out_ref[...] = s_ref[...]


def score_kernel(ex_count, per_dev, a_ref, b_ref, c_ref, d_ref, q_ref, out_ref):
    summed = (a_ref[...] + b_ref[...]) + (c_ref[...] + d_ref[...])
    total = summed.shape[1]
    z = lax.axis_index("ex")
    q = q_ref[...]
    place = jnp.bitwise_xor(q // per_dev, z) * per_dev + q % per_dev
    rows = lax.broadcasted_iota(jnp.int32, (total, q.shape[1]), 0)
    chosen = jnp.where(rows == place, 1.0, 0.0).astype(BF16)
    hi, mid, low = split3(summed)
    out_ref[...] = (nn(low, chosen) + nn(mid, chosen)) + nn(hi, chosen)


def vmem():
    return pl.BlockSpec(memory_space=pltpu.VMEM)


def swap(x, axis, count, k):
    return lax.ppermute(x, axis, [(i, i ^ k) for i in range(count)])


def small_device(ex_count, layer_count, layer_inputs, out_grads, proj_in, proj_out, frame_lengths, query_ids):
    frames = layer_inputs.shape[1]
    rank = proj_in.shape[2]
    per_dev = frame_lengths.shape[1]
    total = ex_count * per_dev
    hbm = pl.BlockSpec(memory_space=pltpu.HBM)
    packet = pl.pallas_call(
        project_kernel,
        out_shape=jax.ShapeDtypeStruct((2 * rank + 8, frames), F32),
        in_specs=[hbm] * 5,
        out_specs=vmem(),
        scratch_shapes=[
            pltpu.SMEM(frame_lengths.shape, jnp.int32),
            pltpu.VMEM(layer_inputs.shape[1:], BF16),
            pltpu.VMEM(out_grads.shape[1:], BF16),
            pltpu.VMEM((rank, proj_in.shape[1]), BF16),
            pltpu.VMEM((rank, proj_out.shape[1]), BF16),
            pltpu.SemaphoreType.DMA((4 + CHUNKS,)),
        ],
        compiler_params=pltpu.CompilerParams(vmem_limit_bytes=56508416),
        name="project",
    )(frame_lengths, layer_inputs, out_grads, jnp.swapaxes(proj_in, 1, 2), jnp.swapaxes(proj_out, 1, 2))
    packets = [packet] + [swap(packet, "ex", ex_count, k) for k in range(1, ex_count)]
    share = pl.pallas_call(
        functools.partial(solve_kernel, rank * rank, per_dev, rank),
        out_shape=jax.ShapeDtypeStruct((per_dev, total), F32),
        in_specs=[vmem()] * ex_count,
        out_specs=vmem(),
        scratch_shapes=[pltpu.VMEM((per_dev, total), F32)],
        compiler_params=pltpu.CompilerParams(vmem_limit_bytes=16 * 1024 * 1024),
        name="solve",
    )(*packets)
    shares = [share] + [swap(share, "layer", layer_count, k) for k in range(1, layer_count)]
    scores = pl.pallas_call(
        functools.partial(score_kernel, ex_count, per_dev),
        out_shape=jax.ShapeDtypeStruct((per_dev, query_ids.shape[0]), F32),
        in_specs=[vmem()] * 5,
        out_specs=vmem(),
        compiler_params=pltpu.CompilerParams(vmem_limit_bytes=16 * 1024 * 1024),
        name="score",
    )(*shares, query_ids.reshape(1, -1))
    return scores.T


def large_device(layer_inputs, out_grads, proj_in, proj_out, frame_lengths, query_ids):
    frame_count = layer_inputs.shape[1]
    in_proj = jnp.dot(layer_inputs[0], proj_in[0], preferred_element_type=F32)
    out_proj = jnp.dot(out_grads[0], proj_out[0], preferred_element_type=F32)
    rank = in_proj.shape[1]
    width = rank * rank
    outer_terms = (out_proj[:, :, None] * in_proj[:, None, :]).reshape(frame_count, width)
    lengths = frame_lengths[0]
    end_frames = jnp.cumsum(lengths)
    starts = end_frames - lengths
    positions = jnp.arange(frame_count, dtype=jnp.int32)
    member = ((positions[None, :] >= starts[:, None]) & (positions[None, :] < end_frames[:, None])).astype(F32)
    features = jnp.dot(member, outer_terms, precision=lax.Precision.HIGHEST)
    all_features = lax.all_gather(features, "ex", axis=0, tiled=True)
    count = all_features.shape[0]
    kernel = lax.dot_general(
        all_features, all_features, (((1,), (1,)), ((), ())), precision=lax.Precision.HIGHEST, preferred_element_type=F32
    )
    damping = 0.1 * jnp.trace(kernel) / width
    factor = jnp.linalg.cholesky(kernel + damping * jnp.eye(count, dtype=F32))
    mine = lax.axis_index("ex") * lengths.shape[0] + jnp.arange(lengths.shape[0])
    picked = (jnp.arange(count)[:, None] == mine[None, :]).astype(F32)
    share = picked - damping * jax.scipy.linalg.cho_solve((factor, True), picked)
    summed = lax.psum(share, "layer")
    chosen = (query_ids[:, None] == jnp.arange(count, dtype=jnp.int32)[None, :]).astype(F32)
    return jnp.dot(chosen, summed, precision=lax.Precision.HIGHEST)


def solution(mesh):
    ex_count, layer_count = mesh.shape["ex"], mesh.shape["layer"]
    if ex_count == 4 and layer_count == 4:
        per_device = functools.partial(small_device, ex_count, layer_count)
    else:
        per_device = large_device
    return jax.shard_map(
        per_device,
        mesh=mesh,
        in_specs=(
            P("layer", ("groups", "ex"), None),
            P("layer", ("groups", "ex"), None),
            P("layer", None, None),
            P("layer", None, None),
            P(("groups", "ex"), None),
            P("groups"),
        ),
        out_specs=P("groups", "ex"),
        check_vma=False,
    )
```

```python
import functools

import jax
import jax.numpy as jnp
from jax import lax
from jax.experimental import pallas as pl
from jax.experimental.pallas import tpu as pltpu
from jax.sharding import PartitionSpec as P

F32 = jnp.float32
BF16 = jnp.bfloat16
CHUNKS = 4
RING = (0, 2, 1, 3)
HOPS = (0, 2, 3, 1)


def nt(a, b):
    return lax.dot_general(a, b, (((1,), (1,)), ((), ())), preferred_element_type=F32)


def nn(a, b):
    return lax.dot_general(a, b, (((1,), (0,)), ((), ())), preferred_element_type=F32)


def tn(a, b):
    return lax.dot_general(a, b, (((0,), (0,)), ((), ())), preferred_element_type=F32)


def split3(x):
    hi = x.astype(BF16)
    rest = x - hi.astype(F32)
    mid = rest.astype(BF16)
    low = (rest - mid.astype(F32)).astype(BF16)
    return hi, mid, low


def split2(x):
    hi = x.astype(BF16)
    return hi, (x - hi.astype(F32)).astype(BF16)


def mm(a, b):
    ah, al = split2(a)
    bh, bl = split2(b)
    return nn(ah, bh) + (nn(ah, bl) + nn(al, bh))


def exact(a, b, dims):
    return lax.dot_general(a, b, (dims, ((), ())), precision=lax.Precision.HIGHEST, preferred_element_type=F32)


def project_kernel(lens_hbm, li_ref, og_ref, pi_ref, po_ref, out_ref, lens_ref, li_v, og_v, pi_v, po_v, sems):
    ff = og_ref.shape[2]
    step = ff // CHUNKS
    copies = [
        pltpu.make_async_copy(pi_ref.at[0], pi_v, sems.at[0]),
        pltpu.make_async_copy(li_ref.at[0], li_v, sems.at[1]),
        pltpu.make_async_copy(po_ref.at[0], po_v, sems.at[2]),
        pltpu.make_async_copy(lens_hbm, lens_ref, sems.at[3]),
    ]
    for c in range(CHUNKS):
        cols = pl.ds(c * step, step)
        copies.append(pltpu.make_async_copy(og_ref.at[0, :, cols], og_v.at[:, cols], sems.at[4 + c]))
    for copy in copies:
        copy.start()
    rank = pi_ref.shape[1]
    frames = li_ref.shape[1]
    positions = lax.broadcasted_iota(jnp.int32, (8, frames), 1)
    copies[3].wait()
    ids = jnp.zeros((8, frames), F32)
    end = lens_ref[0, 0]
    for j in range(1, lens_ref.shape[1]):
        ids = ids + jnp.where(positions >= end, 1.0, 0.0)
        end = end + lens_ref[0, j]
    out_ref[2 * rank:, :] = ids
    copies[0].wait()
    copies[1].wait()
    out_ref[rank:2 * rank, :] = nt(pi_v[...], li_v[...])
    copies[2].wait()
    total = jnp.zeros((rank, frames), F32)
    for c in range(CHUNKS):
        copies[4 + c].wait()
        total = total + nt(po_v[:, c * step:(c + 1) * step], og_v[:, c * step:(c + 1) * step])
    out_ref[:rank, :] = total


def orthogonal_shares(width, per_dev, rank, packets, member, v_ref):
    total = member.shape[0]
    blocks, lanes = v_ref.shape[0] - 1, v_ref.shape[2]
    per = lanes // rank
    in_proj = jnp.concatenate([jnp.concatenate([p[rank:2 * rank, :] for p in packets], axis=1)] * per, axis=0)
    owner = lax.broadcasted_iota(jnp.int32, in_proj.shape, 0) // rank

    def fill(g, carry):
        block = jnp.zeros((total, lanes), F32)
        for s in range(per):
            out_row = jnp.concatenate([p[pl.ds(g * per + s, 1), :] for p in packets], axis=1)
            block = block + exact(member * out_row, jnp.where(owner == s, in_proj, 0.0), ((1,), (1,)))
        v_ref[pl.ds(g, 1)] = block[None]
        return carry

    lax.fori_loop(0, blocks, fill, 0)
    features = v_ref[:blocks]
    damp = jnp.sum(features * features, keepdims=True)[0] * (0.1 / width)
    row = lax.broadcasted_iota(jnp.int32, (total, lanes), 0)
    lane = lax.broadcasted_iota(jnp.int32, (total, lanes), 1)
    v_ref[blocks] = jnp.where(row == lane, jnp.sqrt(damp), 0.0)

    def step(k, carry):
        v = v_ref[...]
        rows = lax.broadcasted_iota(jnp.int32, v.shape, 1)
        q = jnp.sum(jnp.where(rows == k, v, 0.0), axis=1, keepdims=True)
        size = jnp.sum(jnp.sum(q * q, axis=0, keepdims=True), axis=2, keepdims=True)
        q = q / jnp.sqrt(size)
        along = jnp.sum(jnp.sum(v * q, axis=0, keepdims=True), axis=2, keepdims=True)
        v_ref[...] = jnp.where(rows > k, v - along * q, jnp.where(rows == k, q, v))
        return carry

    lax.fori_loop(0, total, step, 0)
    last = v_ref[blocks]
    inverse = exact(last, last, ((0,), (0,)))
    return jnp.where(row == lane, 1.0, 0.0)[:per_dev, :total] - inverse[:per_dev, :total]


def solve_kernel(width, per_dev, rank, *refs):
    packets, out_ref, s_ref, v_ref = refs[:-3], refs[-3], refs[-2], refs[-1]
    frames = packets[0].shape[1]
    count = len(packets)
    total = count * per_dev

    def terms(lo):
        x = jnp.concatenate([p[lo:lo + rank, :] for p in packets], axis=1)
        hi, low = split2(x)
        return jnp.concatenate([hi, hi, low], axis=0), jnp.concatenate([hi, low, hi], axis=0)

    left_o, right_o = terms(0)
    left_i, right_i = terms(rank)
    row = lax.broadcasted_iota(jnp.int32, (total, frames), 0).astype(F32)
    membership = jnp.concatenate(
        [jnp.where(p[2 * rank:2 * rank + 1, :] + float(k * per_dev) == row, 1.0, 0.0) for k, p in enumerate(packets)], axis=1
    )
    member = membership.astype(BF16)
    hi, low = split2(tn(left_o, right_o) * tn(left_i, right_i))
    hi, low = split2(nt(low, member) + nt(hi, member))
    kernel = nn(member, low) + nn(member, hi)

    ids0 = lax.broadcasted_iota(jnp.int32, (total, total), 0)
    ids1 = lax.broadcasted_iota(jnp.int32, (total, total), 1)
    diagonal = ids0 == ids1
    eye = jnp.where(diagonal, 1.0, 0.0)
    damp = jnp.sum(jnp.where(diagonal, kernel, 0.0), keepdims=True) * (0.1 / width)
    scale = jnp.sum(jnp.where(diagonal, kernel, 0.0), axis=0, keepdims=True) + damp
    ratio = damp / scale
    column = jnp.sum(jnp.where(diagonal, ratio, 0.0), axis=1, keepdims=True)
    e1 = jnp.where(diagonal, 0.0, -kernel / scale)
    mine = e1[:per_dev] + eye[:per_dev]
    e2 = mm(e1, e1)
    mine = mine + mm(mine, e2)
    e4 = mm(e2, e2)
    mine = mine + mm(mine, e4)
    e8 = mm(e4, e4)
    mine = mine + mm(mine, e8)
    squares = e8 * e8
    left = jnp.sum(squares * column)
    spread = jnp.sum(squares * column * (scale / damp))
    good = (left <= 1e-5) & (spread <= 0.005)
    s_ref[...] = eye[:per_dev] - column[:per_dev] * mine

    @pl.when(jnp.logical_not(good))
    def _():
        e16 = mm(e8, e8)
        s_ref[...] = eye[:per_dev] - column[:per_dev] * (mine + mm(mine, e16))
        near = (jnp.sum(e16 * e16 * column) <= 1e-5) & (spread <= 0.05)

        @pl.when(jnp.logical_not(near))
        def _():
            s_ref[...] = orthogonal_shares(width, per_dev, rank, packets, membership, v_ref)

    out_ref[...] = s_ref[...]


def score_kernel(per_dev, a_ref, b_ref, c_ref, d_ref, q_ref, out_ref):
    summed = (a_ref[...] + b_ref[...]) + (c_ref[...] + d_ref[...])
    total = summed.shape[1]
    q = q_ref[...]
    hops = (place_of(lax.axis_index("ex")) - place_of(q // per_dev) + len(RING)) % len(RING)
    slot = jnp.zeros_like(hops)
    for k, h in enumerate(HOPS):
        slot = jnp.where(hops == h, k, slot)
    place = slot * per_dev + q % per_dev
    rows = lax.broadcasted_iota(jnp.int32, (total, q.shape[1]), 0)
    chosen = jnp.where(rows == place, 1.0, 0.0).astype(BF16)
    hi, mid, low = split3(summed)
    out_ref[...] = (nn(low, chosen) + nn(mid, chosen)) + nn(hi, chosen)


def vmem():
    return pl.BlockSpec(memory_space=pltpu.VMEM)


def place_of(index):
    return (index % 2) * 2 + index // 2


def shift(x, hops):
    return lax.ppermute(x, "ex", [(RING[i], RING[(i + hops) % len(RING)]) for i in range(len(RING))])


def swap(x, axis, count, k):
    return lax.ppermute(x, axis, [(i, i ^ k) for i in range(count)])


def small_device(ex_count, layer_count, layer_inputs, out_grads, proj_in, proj_out, frame_lengths, query_ids):
    frames = layer_inputs.shape[1]
    rank = proj_in.shape[2]
    per_dev = frame_lengths.shape[1]
    total = ex_count * per_dev
    hbm = pl.BlockSpec(memory_space=pltpu.HBM)
    packet = pl.pallas_call(
        project_kernel,
        out_shape=jax.ShapeDtypeStruct((2 * rank + 8, frames), F32),
        in_specs=[hbm] * 5,
        out_specs=vmem(),
        scratch_shapes=[
            pltpu.SMEM(frame_lengths.shape, jnp.int32),
            pltpu.VMEM(layer_inputs.shape[1:], BF16),
            pltpu.VMEM(out_grads.shape[1:], BF16),
            pltpu.VMEM((rank, proj_in.shape[1]), BF16),
            pltpu.VMEM((rank, proj_out.shape[1]), BF16),
            pltpu.SemaphoreType.DMA((4 + CHUNKS,)),
        ],
        compiler_params=pltpu.CompilerParams(vmem_limit_bytes=16 * 1024 * 1024),
        name="project",
    )(*[
        pltpu.with_memory_space_constraint(x, pltpu.HBM)
        for x in (frame_lengths, layer_inputs, out_grads, jnp.swapaxes(proj_in, 1, 2), jnp.swapaxes(proj_out, 1, 2))
    ])
    packets = [packet] + [shift(packet, hops) for hops in HOPS[1:]]
    share = pl.pallas_call(
        functools.partial(solve_kernel, rank * rank, per_dev, rank),
        out_shape=jax.ShapeDtypeStruct((per_dev, total), F32),
        in_specs=[vmem()] * ex_count,
        out_specs=vmem(),
        scratch_shapes=[pltpu.VMEM((per_dev, total), F32), pltpu.VMEM((rank * rank // 128 + 1, total, 128), F32)],
        compiler_params=pltpu.CompilerParams(vmem_limit_bytes=16 * 1024 * 1024),
        name="solve",
    )(*packets)
    shares = [share] + [swap(share, "layer", layer_count, k) for k in range(1, layer_count)]
    scores = pl.pallas_call(
        functools.partial(score_kernel, per_dev),
        out_shape=jax.ShapeDtypeStruct((per_dev, query_ids.shape[0]), F32),
        in_specs=[vmem()] * 5,
        out_specs=vmem(),
        compiler_params=pltpu.CompilerParams(vmem_limit_bytes=16 * 1024 * 1024),
        name="score",
    )(*shares, query_ids.reshape(1, -1))
    return scores.T


def large_device(layer_inputs, out_grads, proj_in, proj_out, frame_lengths, query_ids):
    frame_count = layer_inputs.shape[1]
    in_proj = jnp.dot(layer_inputs[0], proj_in[0], preferred_element_type=F32)
    out_proj = jnp.dot(out_grads[0], proj_out[0], preferred_element_type=F32)
    rank = in_proj.shape[1]
    width = rank * rank
    outer_terms = (out_proj[:, :, None] * in_proj[:, None, :]).reshape(frame_count, width)
    lengths = frame_lengths[0]
    end_frames = jnp.cumsum(lengths)
    starts = end_frames - lengths
    positions = jnp.arange(frame_count, dtype=jnp.int32)
    member = ((positions[None, :] >= starts[:, None]) & (positions[None, :] < end_frames[:, None])).astype(F32)
    features = jnp.dot(member, outer_terms, precision=lax.Precision.HIGHEST)
    all_features = lax.all_gather(features, "ex", axis=0, tiled=True)
    count = all_features.shape[0]
    kernel = lax.dot_general(
        all_features, all_features, (((1,), (1,)), ((), ())), precision=lax.Precision.HIGHEST, preferred_element_type=F32
    )
    damping = 0.1 * jnp.trace(kernel) / width
    factor = jnp.linalg.cholesky(kernel + damping * jnp.eye(count, dtype=F32))
    mine = lax.axis_index("ex") * lengths.shape[0] + jnp.arange(lengths.shape[0])
    picked = (jnp.arange(count)[:, None] == mine[None, :]).astype(F32)
    share = picked - damping * jax.scipy.linalg.cho_solve((factor, True), picked)
    summed = lax.psum(share, "layer")
    chosen = (query_ids[:, None] == jnp.arange(count, dtype=jnp.int32)[None, :]).astype(F32)
    return jnp.dot(chosen, summed, precision=lax.Precision.HIGHEST)


def solution(mesh):
    ex_count, layer_count = mesh.shape["ex"], mesh.shape["layer"]
    if ex_count == 4 and layer_count == 4:
        per_device = functools.partial(small_device, ex_count, layer_count)
    else:
        per_device = large_device
    return jax.shard_map(
        per_device,
        mesh=mesh,
        in_specs=(
            P("layer", ("groups", "ex"), None),
            P("layer", ("groups", "ex"), None),
            P("layer", None, None),
            P("layer", None, None),
            P(("groups", "ex"), None),
            P("groups"),
        ),
        out_specs=P("groups", "ex"),
        check_vma=False,
    )
```

```python
import functools

import jax
import jax.numpy as jnp
from jax import lax
from jax.experimental import pallas as pl
from jax.experimental.pallas import tpu as pltpu
from jax.sharding import PartitionSpec as P

F32 = jnp.float32
BF16 = jnp.bfloat16
CHUNKS = 4
RING = (0, 2, 1, 3)
HOPS = (0, 1, 2, 3)
EARLY = 2


def nt(a, b):
    return lax.dot_general(a, b, (((1,), (1,)), ((), ())), preferred_element_type=F32)


def nn(a, b):
    return lax.dot_general(a, b, (((1,), (0,)), ((), ())), preferred_element_type=F32)


def tn(a, b):
    return lax.dot_general(a, b, (((0,), (0,)), ((), ())), preferred_element_type=F32)


def split3(x):
    hi = x.astype(BF16)
    rest = x - hi.astype(F32)
    mid = rest.astype(BF16)
    low = (rest - mid.astype(F32)).astype(BF16)
    return hi, mid, low


def split2(x):
    hi = x.astype(BF16)
    return hi, (x - hi.astype(F32)).astype(BF16)


def mm(a, b):
    ah, al = split2(a)
    bh, bl = split2(b)
    return nn(ah, bh) + (nn(ah, bl) + nn(al, bh))


def exact(a, b, dims):
    return lax.dot_general(a, b, (dims, ((), ())), precision=lax.Precision.HIGHEST, preferred_element_type=F32)


def project_kernel(lens_hbm, li_ref, og_ref, pi_ref, po_ref, out_ref, lens_ref, li_v, og_v, pi_v, po_v, sems):
    ff = og_ref.shape[2]
    step = ff // CHUNKS
    copies = [
        pltpu.make_async_copy(pi_ref.at[0], pi_v, sems.at[0]),
        pltpu.make_async_copy(li_ref.at[0], li_v, sems.at[1]),
        pltpu.make_async_copy(po_ref.at[0], po_v, sems.at[2]),
        pltpu.make_async_copy(lens_hbm, lens_ref, sems.at[3]),
    ]
    for c in range(CHUNKS):
        cols = pl.ds(c * step, step)
        copies.append(pltpu.make_async_copy(og_ref.at[0, :, cols], og_v.at[:, cols], sems.at[4 + c]))
    for copy in copies:
        copy.start()
    rank = pi_ref.shape[1]
    frames = li_ref.shape[1]
    positions = lax.broadcasted_iota(jnp.int32, (8, frames), 1)
    copies[3].wait()
    ids = jnp.zeros((8, frames), F32)
    end = lens_ref[0, 0]
    for j in range(1, lens_ref.shape[1]):
        ids = ids + jnp.where(positions >= end, 1.0, 0.0)
        end = end + lens_ref[0, j]
    out_ref[2 * rank:, :] = ids
    copies[0].wait()
    copies[1].wait()
    out_ref[rank:2 * rank, :] = nt(pi_v[...], li_v[...])
    copies[2].wait()
    total = jnp.zeros((rank, frames), F32)
    for c in range(CHUNKS):
        copies[4 + c].wait()
        total = total + nt(po_v[:, c * step:(c + 1) * step], og_v[:, c * step:(c + 1) * step])
    out_ref[:rank, :] = total


def orthogonal_shares(width, per_dev, rank, packets, member, v_ref):
    total = member.shape[0]
    blocks, lanes = v_ref.shape[0] - 1, v_ref.shape[2]
    per = lanes // rank
    in_proj = jnp.concatenate([jnp.concatenate([p[rank:2 * rank, :] for p in packets], axis=1)] * per, axis=0)
    owner = lax.broadcasted_iota(jnp.int32, in_proj.shape, 0) // rank

    def fill(g, carry):
        block = jnp.zeros((total, lanes), F32)
        for s in range(per):
            out_row = jnp.concatenate([p[pl.ds(g * per + s, 1), :] for p in packets], axis=1)
            block = block + exact(member * out_row, jnp.where(owner == s, in_proj, 0.0), ((1,), (1,)))
        v_ref[pl.ds(g, 1)] = block[None]
        return carry

    lax.fori_loop(0, blocks, fill, 0)
    features = v_ref[:blocks]
    damp = jnp.sum(features * features, keepdims=True)[0] * (0.1 / width)
    row = lax.broadcasted_iota(jnp.int32, (total, lanes), 0)
    lane = lax.broadcasted_iota(jnp.int32, (total, lanes), 1)
    v_ref[blocks] = jnp.where(row == lane, jnp.sqrt(damp), 0.0)

    def step(k, carry):
        v = v_ref[...]
        rows = lax.broadcasted_iota(jnp.int32, v.shape, 1)
        q = jnp.sum(jnp.where(rows == k, v, 0.0), axis=1, keepdims=True)
        size = jnp.sum(jnp.sum(q * q, axis=0, keepdims=True), axis=2, keepdims=True)
        q = q / jnp.sqrt(size)
        along = jnp.sum(jnp.sum(v * q, axis=0, keepdims=True), axis=2, keepdims=True)
        v_ref[...] = jnp.where(rows > k, v - along * q, jnp.where(rows == k, q, v))
        return carry

    lax.fori_loop(0, total, step, 0)
    last = v_ref[blocks]
    inverse = exact(last, last, ((0,), (0,)))
    return jnp.where(row == lane, 1.0, 0.0)[:per_dev, :total] - inverse[:per_dev, :total]


def terms(packets, lo, rank):
    hi, low = split2(jnp.concatenate([p[lo:lo + rank, :] for p in packets], axis=1))
    return jnp.concatenate([hi, hi, low], axis=0), jnp.concatenate([hi, low, hi], axis=0)


def members(packet, first, total, rank):
    row = lax.broadcasted_iota(jnp.int32, (total, packet.shape[1]), 0).astype(F32)
    return jnp.where(packet[2 * rank:2 * rank + 1, :] + float(first) == row, 1.0, 0.0)


def early_kernel(per_dev, rank, query_ref, *refs):
    packets, (out_ref, chosen_ref, left_o_ref, left_i_ref) = refs[:-4], refs[-4:]
    total = out_ref.shape[0]
    chosen_ref[...] = chosen_of(total, per_dev, query_ref[...])
    member = jnp.concatenate([members(p, k * per_dev, total, rank) for k, p in enumerate(packets)], axis=1).astype(BF16)
    left_o, right_o = terms(packets, 0, rank)
    left_i, right_i = terms(packets, rank, rank)
    left_o, left_i = left_o.T, left_i.T
    left_o_ref[...] = left_o
    left_i_ref[...] = left_i
    hi, low = split2(nn(left_o, right_o) * nn(left_i, right_i))
    hi, low = split2(nn(member, low) + nn(member, hi))
    out_ref[...] = nt(low, member) + nt(hi, member)


def extend(known, left_o, left_i, packets, member, skip, rank):
    frames = packets[0].shape[1]
    first, late = member[:, :skip * frames], member[:, skip * frames:]
    late_o, right_o = terms(packets[skip:], 0, rank)
    late_i, right_i = terms(packets[skip:], rank, rank)
    cross_hi, cross_low = split2(nn(left_o, right_o) * nn(left_i, right_i))
    own_hi, own_low = split2(tn(late_o, right_o) * tn(late_i, right_i))
    cross = nn(first, cross_low) + nn(first, cross_hi)
    hi, low = split2(cross + (nn(late, own_low) + nn(late, own_hi)))
    columns = nt(low, late) + nt(hi, late)
    hi, low = split2(cross)
    return known + (columns + (nt(late, low) + nt(late, hi)))


def solve_kernel(width, per_dev, rank, *refs):
    early_ref, left_o_ref, left_i_ref = refs[:3]
    packets, (out_ref, s_ref, v_ref) = refs[3:-3], refs[-3:]
    frames = packets[0].shape[1]
    count = len(packets)
    total = count * per_dev

    membership = jnp.concatenate([members(p, k * per_dev, total, rank) for k, p in enumerate(packets)], axis=1)
    member = membership.astype(BF16)
    kernel = extend(early_ref[...], left_o_ref[...], left_i_ref[...], packets, member, EARLY, rank)

    ids0 = lax.broadcasted_iota(jnp.int32, (total, total), 0)
    ids1 = lax.broadcasted_iota(jnp.int32, (total, total), 1)
    diagonal = ids0 == ids1
    eye = jnp.where(diagonal, 1.0, 0.0)
    damp = jnp.sum(jnp.where(diagonal, kernel, 0.0), keepdims=True) * (0.1 / width)
    scale = jnp.sum(jnp.where(diagonal, kernel, 0.0), axis=0, keepdims=True) + damp
    ratio = damp / scale
    column = jnp.sum(jnp.where(diagonal, ratio, 0.0), axis=1, keepdims=True)
    e1 = jnp.where(diagonal, 0.0, -kernel / scale)
    mine = e1[:per_dev] + eye[:per_dev]
    e2 = mm(e1, e1)
    mine = mine + mm(mine, e2)
    e4 = mm(e2, e2)
    mine = mine + mm(mine, e4)
    e8 = mm(e4, e4)
    mine = mine + mm(mine, e8)
    squares = e8 * e8
    left = jnp.sum(squares * column)
    spread = jnp.sum(squares * column * (scale / damp))
    good = (left <= 1e-5) & (spread <= 0.005)
    s_ref[...] = eye[:per_dev] - column[:per_dev] * mine

    @pl.when(jnp.logical_not(good))
    def _():
        e16 = mm(e8, e8)
        s_ref[...] = eye[:per_dev] - column[:per_dev] * (mine + mm(mine, e16))
        near = (jnp.sum(e16 * e16 * column) <= 1e-5) & (spread <= 0.05)

        @pl.when(jnp.logical_not(near))
        def _():
            s_ref[...] = orthogonal_shares(width, per_dev, rank, packets, membership, v_ref)

    out_ref[...] = s_ref[...]


def chosen_of(total, per_dev, q):
    hops = (place_of(lax.axis_index("ex")) - place_of(q // per_dev) + len(RING)) % len(RING)
    slot = jnp.zeros_like(hops)
    for k, h in enumerate(HOPS):
        slot = jnp.where(hops == h, k, slot)
    place = slot * per_dev + q % per_dev
    rows = lax.broadcasted_iota(jnp.int32, (total, q.shape[1]), 0)
    return jnp.where(rows == place, 1.0, 0.0).astype(BF16)


def score_kernel(a_ref, b_ref, c_ref, d_ref, chosen_ref, out_ref):
    chosen = chosen_ref[...]
    hi, mid, low = split3((a_ref[...] + b_ref[...]) + (c_ref[...] + d_ref[...]))
    out_ref[...] = (nn(low, chosen) + nn(mid, chosen)) + nn(hi, chosen)


def vmem():
    return pl.BlockSpec(memory_space=pltpu.VMEM)


def place_of(index):
    return (index % 2) * 2 + index // 2


def shift(x, hops):
    return lax.ppermute(x, "ex", [(RING[i], RING[(i + hops) % len(RING)]) for i in range(len(RING))])


def swap(x, axis, count, k):
    return lax.ppermute(x, axis, [(i, i ^ k) for i in range(count)])


def small_device(ex_count, layer_count, layer_inputs, out_grads, proj_in, proj_out, frame_lengths, query_ids):
    frames = layer_inputs.shape[1]
    rank = proj_in.shape[2]
    per_dev = frame_lengths.shape[1]
    total = ex_count * per_dev
    hbm = pl.BlockSpec(memory_space=pltpu.HBM)
    packet = pl.pallas_call(
        project_kernel,
        out_shape=jax.ShapeDtypeStruct((2 * rank + 8, frames), F32),
        in_specs=[hbm] * 5,
        out_specs=vmem(),
        scratch_shapes=[
            pltpu.SMEM(frame_lengths.shape, jnp.int32),
            pltpu.VMEM(layer_inputs.shape[1:], BF16),
            pltpu.VMEM(out_grads.shape[1:], BF16),
            pltpu.VMEM((rank, proj_in.shape[1]), BF16),
            pltpu.VMEM((rank, proj_out.shape[1]), BF16),
            pltpu.SemaphoreType.DMA((4 + CHUNKS,)),
        ],
        compiler_params=pltpu.CompilerParams(vmem_limit_bytes=16 * 1024 * 1024),
        name="project",
    )(*[
        pltpu.with_memory_space_constraint(x, pltpu.HBM)
        for x in (frame_lengths, layer_inputs, out_grads, jnp.swapaxes(proj_in, 1, 2), jnp.swapaxes(proj_out, 1, 2))
    ])
    packets = [packet] + [shift(packet, hops) for hops in HOPS[1:]]
    lefts = jax.ShapeDtypeStruct((EARLY * frames, 3 * rank), BF16)
    early, chosen, left_o, left_i = pl.pallas_call(
        functools.partial(early_kernel, per_dev, rank),
        out_shape=(jax.ShapeDtypeStruct((total, total), F32), jax.ShapeDtypeStruct((total, query_ids.shape[0]), BF16), lefts, lefts),
        in_specs=[vmem()] * (1 + EARLY),
        out_specs=(vmem(),) * 4,
        compiler_params=pltpu.CompilerParams(vmem_limit_bytes=16 * 1024 * 1024),
        cost_estimate=pl.CostEstimate(flops=10**6, bytes_accessed=10**5, transcendentals=0),
        name="early",
    )(query_ids.reshape(1, -1), *packets[:EARLY])
    share = pl.pallas_call(
        functools.partial(solve_kernel, rank * rank, per_dev, rank),
        out_shape=jax.ShapeDtypeStruct((per_dev, total), F32),
        in_specs=[vmem()] * (ex_count + 3),
        out_specs=vmem(),
        scratch_shapes=[pltpu.VMEM((per_dev, total), F32), pltpu.VMEM((rank * rank // 128 + 1, total, 128), F32)],
        compiler_params=pltpu.CompilerParams(vmem_limit_bytes=16 * 1024 * 1024),
        name="solve",
    )(early, left_o, left_i, *packets)
    shares = [share] + [swap(share, "layer", layer_count, k) for k in range(1, layer_count)]
    scores = pl.pallas_call(
        score_kernel,
        out_shape=jax.ShapeDtypeStruct((per_dev, query_ids.shape[0]), F32),
        in_specs=[vmem()] * 5,
        out_specs=vmem(),
        compiler_params=pltpu.CompilerParams(vmem_limit_bytes=16 * 1024 * 1024),
        name="score",
    )(*shares, chosen)
    return scores.T


def large_device(layer_inputs, out_grads, proj_in, proj_out, frame_lengths, query_ids):
    frame_count = layer_inputs.shape[1]
    in_proj = jnp.dot(layer_inputs[0], proj_in[0], preferred_element_type=F32)
    out_proj = jnp.dot(out_grads[0], proj_out[0], preferred_element_type=F32)
    rank = in_proj.shape[1]
    width = rank * rank
    outer_terms = (out_proj[:, :, None] * in_proj[:, None, :]).reshape(frame_count, width)
    lengths = frame_lengths[0]
    end_frames = jnp.cumsum(lengths)
    starts = end_frames - lengths
    positions = jnp.arange(frame_count, dtype=jnp.int32)
    member = ((positions[None, :] >= starts[:, None]) & (positions[None, :] < end_frames[:, None])).astype(F32)
    features = jnp.dot(member, outer_terms, precision=lax.Precision.HIGHEST)
    all_features = lax.all_gather(features, "ex", axis=0, tiled=True)
    count = all_features.shape[0]
    kernel = lax.dot_general(
        all_features, all_features, (((1,), (1,)), ((), ())), precision=lax.Precision.HIGHEST, preferred_element_type=F32
    )
    damping = 0.1 * jnp.trace(kernel) / width
    factor = jnp.linalg.cholesky(kernel + damping * jnp.eye(count, dtype=F32))
    mine = lax.axis_index("ex") * lengths.shape[0] + jnp.arange(lengths.shape[0])
    picked = (jnp.arange(count)[:, None] == mine[None, :]).astype(F32)
    share = picked - damping * jax.scipy.linalg.cho_solve((factor, True), picked)
    summed = lax.psum(share, "layer")
    chosen = (query_ids[:, None] == jnp.arange(count, dtype=jnp.int32)[None, :]).astype(F32)
    return jnp.dot(chosen, summed, precision=lax.Precision.HIGHEST)


def solution(mesh):
    ex_count, layer_count = mesh.shape["ex"], mesh.shape["layer"]
    if ex_count == 4 and layer_count == 4:
        per_device = functools.partial(small_device, ex_count, layer_count)
    else:
        per_device = large_device
    return jax.shard_map(
        per_device,
        mesh=mesh,
        in_specs=(
            P("layer", ("groups", "ex"), None),
            P("layer", ("groups", "ex"), None),
            P("layer", None, None),
            P("layer", None, None),
            P(("groups", "ex"), None),
            P("groups"),
        ),
        out_specs=P("groups", "ex"),
        check_vma=False,
    )
```

```python
import functools

import jax
import jax.numpy as jnp
from jax import lax
from jax.experimental import pallas as pl
from jax.experimental.pallas import tpu as pltpu
from jax.sharding import PartitionSpec as P

F32 = jnp.float32
BF16 = jnp.bfloat16
CHUNKS = 4
RING = (0, 2, 1, 3)
HOPS = (0, 1, 2, 3)
EARLY = 2


def nt(a, b):
    return lax.dot_general(a, b, (((1,), (1,)), ((), ())), preferred_element_type=F32)


def nn(a, b):
    return lax.dot_general(a, b, (((1,), (0,)), ((), ())), preferred_element_type=F32)


def tn(a, b):
    return lax.dot_general(a, b, (((0,), (0,)), ((), ())), preferred_element_type=F32)


def split3(x):
    hi = x.astype(BF16)
    rest = x - hi.astype(F32)
    mid = rest.astype(BF16)
    low = (rest - mid.astype(F32)).astype(BF16)
    return hi, mid, low


def split2(x):
    hi = x.astype(BF16)
    return hi, (x - hi.astype(F32)).astype(BF16)


def mm(a, b):
    ah, al = split2(a)
    bh, bl = split2(b)
    return (nn(ah, bl) + nn(al, bh)) + nn(ah, bh)


def exact(a, b, dims):
    return lax.dot_general(a, b, (dims, ((), ())), precision=lax.Precision.HIGHEST, preferred_element_type=F32)


def project_kernel(lens_hbm, li_ref, og_ref, pi_ref, po_ref, out_ref, lens_ref, li_v, og_v, pi_v, po_v, sems):
    ff = og_ref.shape[2]
    step = ff // CHUNKS
    copies = [
        pltpu.make_async_copy(pi_ref.at[0], pi_v, sems.at[0]),
        pltpu.make_async_copy(li_ref.at[0], li_v, sems.at[1]),
        pltpu.make_async_copy(po_ref.at[0], po_v, sems.at[2]),
        pltpu.make_async_copy(lens_hbm, lens_ref, sems.at[3]),
    ]
    for c in range(CHUNKS):
        cols = pl.ds(c * step, step)
        copies.append(pltpu.make_async_copy(og_ref.at[0, :, cols], og_v.at[:, cols], sems.at[4 + c]))
    for copy in copies:
        copy.start()
    rank = pi_ref.shape[1]
    frames = li_ref.shape[1]
    positions = lax.broadcasted_iota(jnp.int32, (8, frames), 1)
    copies[3].wait()
    ids = jnp.zeros((8, frames), F32)
    end = lens_ref[0, 0]
    for j in range(1, lens_ref.shape[1]):
        ids = ids + jnp.where(positions >= end, 1.0, 0.0)
        end = end + lens_ref[0, j]
    out_ref[2 * rank:, :] = ids
    copies[0].wait()
    copies[1].wait()
    out_ref[rank:2 * rank, :] = nt(pi_v[...], li_v[...])
    copies[2].wait()
    total = jnp.zeros((rank, frames), F32)
    for c in range(CHUNKS):
        copies[4 + c].wait()
        total = total + nt(po_v[:, c * step:(c + 1) * step], og_v[:, c * step:(c + 1) * step])
    out_ref[:rank, :] = total


def orthogonal_shares(width, per_dev, rank, packets, member, v_ref):
    total = member.shape[0]
    blocks, lanes = v_ref.shape[0] - 1, v_ref.shape[2]
    per = lanes // rank
    in_proj = jnp.concatenate([jnp.concatenate([p[rank:2 * rank, :] for p in packets], axis=1)] * per, axis=0)
    owner = lax.broadcasted_iota(jnp.int32, in_proj.shape, 0) // rank

    def fill(g, carry):
        block = jnp.zeros((total, lanes), F32)
        for s in range(per):
            out_row = jnp.concatenate([p[pl.ds(g * per + s, 1), :] for p in packets], axis=1)
            block = block + exact(member * out_row, jnp.where(owner == s, in_proj, 0.0), ((1,), (1,)))
        v_ref[pl.ds(g, 1)] = block[None]
        return carry

    lax.fori_loop(0, blocks, fill, 0)
    features = v_ref[:blocks]
    damp = jnp.sum(features * features, keepdims=True)[0] * (0.1 / width)
    row = lax.broadcasted_iota(jnp.int32, (total, lanes), 0)
    lane = lax.broadcasted_iota(jnp.int32, (total, lanes), 1)
    v_ref[blocks] = jnp.where(row == lane, jnp.sqrt(damp), 0.0)

    def step(k, carry):
        v = v_ref[...]
        rows = lax.broadcasted_iota(jnp.int32, v.shape, 1)
        q = jnp.sum(jnp.where(rows == k, v, 0.0), axis=1, keepdims=True)
        size = jnp.sum(jnp.sum(q * q, axis=0, keepdims=True), axis=2, keepdims=True)
        q = q / jnp.sqrt(size)
        along = jnp.sum(jnp.sum(v * q, axis=0, keepdims=True), axis=2, keepdims=True)
        v_ref[...] = jnp.where(rows > k, v - along * q, jnp.where(rows == k, q, v))
        return carry

    lax.fori_loop(0, total, step, 0)
    last = v_ref[blocks]
    inverse = exact(last, last, ((0,), (0,)))
    return jnp.where(row == lane, 1.0, 0.0)[:per_dev, :total] - inverse[:per_dev, :total]


def terms(packets, lo, rank):
    hi, low = split2(jnp.concatenate([p[lo:lo + rank, :] for p in packets], axis=1))
    return jnp.concatenate([hi, hi, low], axis=0), jnp.concatenate([hi, low, hi], axis=0)


def members(packet, first, total, rank):
    row = lax.broadcasted_iota(jnp.int32, (total, packet.shape[1]), 0).astype(F32)
    return jnp.where(packet[2 * rank:2 * rank + 1, :] + float(first) == row, 1.0, 0.0)


def early_kernel(per_dev, rank, query_ref, *refs):
    packets, (out_ref, chosen_ref, left_o_ref, left_i_ref) = refs[:-4], refs[-4:]
    total = out_ref.shape[0]
    chosen_ref[...] = chosen_of(total, per_dev, query_ref[...])
    member = jnp.concatenate([members(p, k * per_dev, total, rank) for k, p in enumerate(packets)], axis=1).astype(BF16)
    left_o, right_o = terms(packets, 0, rank)
    left_i, right_i = terms(packets, rank, rank)
    left_o, left_i = left_o.T, left_i.T
    left_o_ref[...] = left_o
    left_i_ref[...] = left_i
    hi, low = split2(nn(left_o, right_o) * nn(left_i, right_i))
    hi, low = split2(nn(member, low) + nn(member, hi))
    out_ref[...] = nt(low, member) + nt(hi, member)


def extend(known, left_o, left_i, packets, member, skip, rank):
    frames = packets[0].shape[1]
    first, late = member[:, :skip * frames], member[:, skip * frames:]
    late_o, right_o = terms(packets[skip:], 0, rank)
    late_i, right_i = terms(packets[skip:], rank, rank)
    cross_hi, cross_low = split2(nn(left_o, right_o) * nn(left_i, right_i))
    own_hi, own_low = split2(tn(late_o, right_o) * tn(late_i, right_i))
    cross = nn(first, cross_low) + nn(first, cross_hi)
    hi, low = split2(cross + (nn(late, own_low) + nn(late, own_hi)))
    columns = nt(low, late) + nt(hi, late)
    hi, low = split2(cross)
    return known + (columns + (nt(late, low) + nt(late, hi)))


def solve_kernel(width, per_dev, rank, *refs):
    early_ref, left_o_ref, left_i_ref = refs[:3]
    packets, (out_ref, s_ref, v_ref) = refs[3:-3], refs[-3:]
    frames = packets[0].shape[1]
    count = len(packets)
    total = count * per_dev

    membership = jnp.concatenate([members(p, k * per_dev, total, rank) for k, p in enumerate(packets)], axis=1)
    member = membership.astype(BF16)
    kernel = extend(early_ref[...], left_o_ref[...], left_i_ref[...], packets, member, EARLY, rank)

    ids0 = lax.broadcasted_iota(jnp.int32, (total, total), 0)
    ids1 = lax.broadcasted_iota(jnp.int32, (total, total), 1)
    diagonal = ids0 == ids1
    eye = jnp.where(diagonal, 1.0, 0.0)
    own = jnp.sum(jnp.where(diagonal, kernel, 0.0), axis=0, keepdims=True)
    damp = jnp.sum(own, axis=1, keepdims=True) * (0.1 / width)
    scale = own + damp
    inverse = 1.0 / scale
    column = jnp.sum(jnp.where(diagonal, damp * inverse, 0.0), axis=1, keepdims=True)
    e1 = jnp.where(diagonal, 0.0, kernel) * -inverse
    mine = e1[:per_dev] + eye[:per_dev]
    e2 = mm(e1, e1)
    e4 = mm(e2, e2)
    mine = mine + mm(mine, e2)
    e8 = mm(e4, e4)
    mine = mine + mm(mine, e4)
    mine = mine + mm(mine, e8)
    squares = e8 * e8
    left = jnp.sum(squares * column)
    spread = jnp.sum(squares * column * (scale / damp))
    good = (left <= 1e-5) & (spread <= 0.005)
    s_ref[...] = eye[:per_dev] - column[:per_dev] * mine

    @pl.when(jnp.logical_not(good))
    def _():
        e16 = mm(e8, e8)
        s_ref[...] = eye[:per_dev] - column[:per_dev] * (mine + mm(mine, e16))
        near = (jnp.sum(e16 * e16 * column) <= 1e-5) & (spread <= 0.05)

        @pl.when(jnp.logical_not(near))
        def _():
            s_ref[...] = orthogonal_shares(width, per_dev, rank, packets, membership, v_ref)

    out_ref[...] = s_ref[...]


def chosen_of(total, per_dev, q):
    hops = (place_of(lax.axis_index("ex")) - place_of(q // per_dev) + len(RING)) % len(RING)
    slot = jnp.zeros_like(hops)
    for k, h in enumerate(HOPS):
        slot = jnp.where(hops == h, k, slot)
    place = slot * per_dev + q % per_dev
    rows = lax.broadcasted_iota(jnp.int32, (total, q.shape[1]), 0)
    return jnp.where(rows == place, 1.0, 0.0).astype(BF16)


def score_kernel(a_ref, b_ref, c_ref, d_ref, chosen_ref, out_ref):
    chosen = chosen_ref[...]
    hi, mid, low = split3((a_ref[...] + b_ref[...]) + (c_ref[...] + d_ref[...]))
    out_ref[...] = (nn(low, chosen) + nn(mid, chosen)) + nn(hi, chosen)


def vmem():
    return pl.BlockSpec(memory_space=pltpu.VMEM)


def place_of(index):
    return (index % 2) * 2 + index // 2


def shift(x, hops):
    return lax.ppermute(x, "ex", [(RING[i], RING[(i + hops) % len(RING)]) for i in range(len(RING))])


def swap(x, axis, count, k):
    return lax.ppermute(x, axis, [(i, i ^ k) for i in range(count)])


def small_device(ex_count, layer_count, layer_inputs, out_grads, proj_in, proj_out, frame_lengths, query_ids):
    frames = layer_inputs.shape[1]
    rank = proj_in.shape[2]
    per_dev = frame_lengths.shape[1]
    total = ex_count * per_dev
    hbm = pl.BlockSpec(memory_space=pltpu.HBM)
    packet = pl.pallas_call(
        project_kernel,
        out_shape=jax.ShapeDtypeStruct((2 * rank + 8, frames), F32),
        in_specs=[hbm] * 5,
        out_specs=vmem(),
        scratch_shapes=[
            pltpu.SMEM(frame_lengths.shape, jnp.int32),
            pltpu.VMEM(layer_inputs.shape[1:], BF16),
            pltpu.VMEM(out_grads.shape[1:], BF16),
            pltpu.VMEM((rank, proj_in.shape[1]), BF16),
            pltpu.VMEM((rank, proj_out.shape[1]), BF16),
            pltpu.SemaphoreType.DMA((4 + CHUNKS,)),
        ],
        compiler_params=pltpu.CompilerParams(vmem_limit_bytes=16 * 1024 * 1024),
        name="project",
    )(*[
        pltpu.with_memory_space_constraint(x, pltpu.HBM)
        for x in (frame_lengths, layer_inputs, out_grads, jnp.swapaxes(proj_in, 1, 2), jnp.swapaxes(proj_out, 1, 2))
    ])
    packets = [packet] + [shift(packet, hops) for hops in HOPS[1:]]
    lefts = jax.ShapeDtypeStruct((EARLY * frames, 3 * rank), BF16)
    early, chosen, left_o, left_i = pl.pallas_call(
        functools.partial(early_kernel, per_dev, rank),
        out_shape=(jax.ShapeDtypeStruct((total, total), F32), jax.ShapeDtypeStruct((total, query_ids.shape[0]), BF16), lefts, lefts),
        in_specs=[vmem()] * (1 + EARLY),
        out_specs=(vmem(),) * 4,
        compiler_params=pltpu.CompilerParams(vmem_limit_bytes=16 * 1024 * 1024),
        cost_estimate=pl.CostEstimate(flops=10**6, bytes_accessed=10**5, transcendentals=0),
        name="early",
    )(query_ids.reshape(1, -1), *packets[:EARLY])
    share = pl.pallas_call(
        functools.partial(solve_kernel, rank * rank, per_dev, rank),
        out_shape=jax.ShapeDtypeStruct((per_dev, total), F32),
        in_specs=[vmem()] * (ex_count + 3),
        out_specs=vmem(),
        scratch_shapes=[pltpu.VMEM((per_dev, total), F32), pltpu.VMEM((rank * rank // 128 + 1, total, 128), F32)],
        compiler_params=pltpu.CompilerParams(vmem_limit_bytes=16 * 1024 * 1024),
        name="solve",
    )(early, left_o, left_i, *packets)
    shares = [share] + [swap(share, "layer", layer_count, k) for k in range(1, layer_count)]
    scores = pl.pallas_call(
        score_kernel,
        out_shape=jax.ShapeDtypeStruct((per_dev, query_ids.shape[0]), F32),
        in_specs=[vmem()] * 5,
        out_specs=vmem(),
        compiler_params=pltpu.CompilerParams(vmem_limit_bytes=16 * 1024 * 1024),
        name="score",
    )(*shares, chosen)
    return scores.T


def large_device(layer_inputs, out_grads, proj_in, proj_out, frame_lengths, query_ids):
    frame_count = layer_inputs.shape[1]
    in_proj = jnp.dot(layer_inputs[0], proj_in[0], preferred_element_type=F32)
    out_proj = jnp.dot(out_grads[0], proj_out[0], preferred_element_type=F32)
    rank = in_proj.shape[1]
    width = rank * rank
    outer_terms = (out_proj[:, :, None] * in_proj[:, None, :]).reshape(frame_count, width)
    lengths = frame_lengths[0]
    end_frames = jnp.cumsum(lengths)
    starts = end_frames - lengths
    positions = jnp.arange(frame_count, dtype=jnp.int32)
    member = ((positions[None, :] >= starts[:, None]) & (positions[None, :] < end_frames[:, None])).astype(F32)
    features = jnp.dot(member, outer_terms, precision=lax.Precision.HIGHEST)
    all_features = lax.all_gather(features, "ex", axis=0, tiled=True)
    count = all_features.shape[0]
    kernel = lax.dot_general(
        all_features, all_features, (((1,), (1,)), ((), ())), precision=lax.Precision.HIGHEST, preferred_element_type=F32
    )
    damping = 0.1 * jnp.trace(kernel) / width
    factor = jnp.linalg.cholesky(kernel + damping * jnp.eye(count, dtype=F32))
    mine = lax.axis_index("ex") * lengths.shape[0] + jnp.arange(lengths.shape[0])
    picked = (jnp.arange(count)[:, None] == mine[None, :]).astype(F32)
    share = picked - damping * jax.scipy.linalg.cho_solve((factor, True), picked)
    summed = lax.psum(share, "layer")
    chosen = (query_ids[:, None] == jnp.arange(count, dtype=jnp.int32)[None, :]).astype(F32)
    return jnp.dot(chosen, summed, precision=lax.Precision.HIGHEST)


def solution(mesh):
    ex_count, layer_count = mesh.shape["ex"], mesh.shape["layer"]
    if ex_count == 4 and layer_count == 4:
        per_device = functools.partial(small_device, ex_count, layer_count)
    else:
        per_device = large_device
    return jax.shard_map(
        per_device,
        mesh=mesh,
        in_specs=(
            P("layer", ("groups", "ex"), None),
            P("layer", ("groups", "ex"), None),
            P("layer", None, None),
            P("layer", None, None),
            P(("groups", "ex"), None),
            P("groups"),
        ),
        out_specs=P("groups", "ex"),
        check_vma=False,
    )
```

```python
import functools

import jax
import jax.numpy as jnp
from jax import lax
from jax.experimental import pallas as pl
from jax.experimental.pallas import tpu as pltpu
from jax.sharding import PartitionSpec as P

F32 = jnp.float32
BF16 = jnp.bfloat16
CHUNKS = 4
RING = (0, 2, 1, 3)
HOPS = (0, 1, 2, 3)
EARLY = 2
RELAX = 0.92


def nt(a, b):
    return lax.dot_general(a, b, (((1,), (1,)), ((), ())), preferred_element_type=F32)


def nn(a, b):
    return lax.dot_general(a, b, (((1,), (0,)), ((), ())), preferred_element_type=F32)


def tn(a, b):
    return lax.dot_general(a, b, (((0,), (0,)), ((), ())), preferred_element_type=F32)


def split3(x):
    hi = x.astype(BF16)
    rest = x - hi.astype(F32)
    mid = rest.astype(BF16)
    low = (rest - mid.astype(F32)).astype(BF16)
    return hi, mid, low


def split2(x):
    hi = x.astype(BF16)
    return hi, (x - hi.astype(F32)).astype(BF16)


def mm(a, b):
    ah, al = split2(a)
    bh, bl = split2(b)
    return (nn(ah, bl) + nn(al, bh)) + nn(ah, bh)


def exact(a, b, dims):
    return lax.dot_general(a, b, (dims, ((), ())), precision=lax.Precision.HIGHEST, preferred_element_type=F32)


def project_kernel(lens_hbm, li_ref, og_ref, pi_ref, po_ref, out_ref, lens_ref, li_v, og_v, pi_v, po_v, sems):
    ff = og_ref.shape[2]
    step = ff // CHUNKS
    copies = [
        pltpu.make_async_copy(pi_ref.at[0], pi_v, sems.at[0]),
        pltpu.make_async_copy(li_ref.at[0], li_v, sems.at[1]),
        pltpu.make_async_copy(po_ref.at[0], po_v, sems.at[2]),
        pltpu.make_async_copy(lens_hbm, lens_ref, sems.at[3]),
    ]
    for c in range(CHUNKS):
        cols = pl.ds(c * step, step)
        copies.append(pltpu.make_async_copy(og_ref.at[0, :, cols], og_v.at[:, cols], sems.at[4 + c]))
    for copy in copies:
        copy.start()
    rank = pi_ref.shape[1]
    frames = li_ref.shape[1]
    positions = lax.broadcasted_iota(jnp.int32, (8, frames), 1)
    copies[3].wait()
    ids = jnp.zeros((8, frames), F32)
    end = lens_ref[0, 0]
    for j in range(1, lens_ref.shape[1]):
        ids = ids + jnp.where(positions >= end, 1.0, 0.0)
        end = end + lens_ref[0, j]
    out_ref[2 * rank:, :] = ids
    copies[0].wait()
    copies[1].wait()
    out_ref[rank:2 * rank, :] = nt(pi_v[...], li_v[...])
    copies[2].wait()
    total = jnp.zeros((rank, frames), F32)
    for c in range(CHUNKS):
        copies[4 + c].wait()
        total = total + nt(po_v[:, c * step:(c + 1) * step], og_v[:, c * step:(c + 1) * step])
    out_ref[:rank, :] = total


def orthogonal_shares(width, per_dev, rank, packets, member, v_ref):
    total = member.shape[0]
    blocks, lanes = v_ref.shape[0] - 1, v_ref.shape[2]
    per = lanes // rank
    in_proj = jnp.concatenate([jnp.concatenate([p[rank:2 * rank, :] for p in packets], axis=1)] * per, axis=0)
    owner = lax.broadcasted_iota(jnp.int32, in_proj.shape, 0) // rank

    def fill(g, carry):
        block = jnp.zeros((total, lanes), F32)
        for s in range(per):
            out_row = jnp.concatenate([p[pl.ds(g * per + s, 1), :] for p in packets], axis=1)
            block = block + exact(member * out_row, jnp.where(owner == s, in_proj, 0.0), ((1,), (1,)))
        v_ref[pl.ds(g, 1)] = block[None]
        return carry

    lax.fori_loop(0, blocks, fill, 0)
    features = v_ref[:blocks]
    damp = jnp.sum(features * features, keepdims=True)[0] * (0.1 / width)
    row = lax.broadcasted_iota(jnp.int32, (total, lanes), 0)
    lane = lax.broadcasted_iota(jnp.int32, (total, lanes), 1)
    v_ref[blocks] = jnp.where(row == lane, jnp.sqrt(damp), 0.0)

    def step(k, carry):
        v = v_ref[...]
        rows = lax.broadcasted_iota(jnp.int32, v.shape, 1)
        q = jnp.sum(jnp.where(rows == k, v, 0.0), axis=1, keepdims=True)
        size = jnp.sum(jnp.sum(q * q, axis=0, keepdims=True), axis=2, keepdims=True)
        q = q / jnp.sqrt(size)
        along = jnp.sum(jnp.sum(v * q, axis=0, keepdims=True), axis=2, keepdims=True)
        v_ref[...] = jnp.where(rows > k, v - along * q, jnp.where(rows == k, q, v))
        return carry

    lax.fori_loop(0, total, step, 0)
    last = v_ref[blocks]
    inverse = exact(last, last, ((0,), (0,)))
    return jnp.where(row == lane, 1.0, 0.0)[:per_dev, :total] - inverse[:per_dev, :total]


def terms(packets, lo, rank):
    hi, low = split2(jnp.concatenate([p[lo:lo + rank, :] for p in packets], axis=1))
    return jnp.concatenate([hi, hi, low], axis=0), jnp.concatenate([hi, low, hi], axis=0)


def members(packet, first, total, rank):
    row = lax.broadcasted_iota(jnp.int32, (total, packet.shape[1]), 0).astype(F32)
    return jnp.where(packet[2 * rank:2 * rank + 1, :] + float(first) == row, 1.0, 0.0)


def early_kernel(per_dev, rank, query_ref, *refs):
    packets, (out_ref, chosen_ref, left_o_ref, left_i_ref) = refs[:-4], refs[-4:]
    total = out_ref.shape[0]
    chosen_ref[...] = chosen_of(total, per_dev, query_ref[...])
    member = jnp.concatenate([members(p, k * per_dev, total, rank) for k, p in enumerate(packets)], axis=1).astype(BF16)
    left_o, right_o = terms(packets, 0, rank)
    left_i, right_i = terms(packets, rank, rank)
    left_o, left_i = left_o.T, left_i.T
    left_o_ref[...] = left_o
    left_i_ref[...] = left_i
    hi, low = split2(nn(left_o, right_o) * nn(left_i, right_i))
    hi, low = split2(nn(member, low) + nn(member, hi))
    out_ref[...] = nt(low, member) + nt(hi, member)


def extend(known, left_o, left_i, packets, member, skip, rank):
    frames = packets[0].shape[1]
    first, late = member[:, :skip * frames], member[:, skip * frames:]
    late_o, right_o = terms(packets[skip:], 0, rank)
    late_i, right_i = terms(packets[skip:], rank, rank)
    cross_hi, cross_low = split2(nn(left_o, right_o) * nn(left_i, right_i))
    own_hi, own_low = split2(tn(late_o, right_o) * tn(late_i, right_i))
    cross = nn(first, cross_low) + nn(first, cross_hi)
    hi, low = split2(cross + (nn(late, own_low) + nn(late, own_hi)))
    columns = nt(low, late) + nt(hi, late)
    hi, low = split2(cross)
    return known + (columns + (nt(late, low) + nt(late, hi)))


def solve_kernel(width, per_dev, rank, *refs):
    early_ref, left_o_ref, left_i_ref = refs[:3]
    packets, (out_ref, s_ref, v_ref) = refs[3:-3], refs[-3:]
    frames = packets[0].shape[1]
    count = len(packets)
    total = count * per_dev

    membership = jnp.concatenate([members(p, k * per_dev, total, rank) for k, p in enumerate(packets)], axis=1)
    member = membership.astype(BF16)
    kernel = extend(early_ref[...], left_o_ref[...], left_i_ref[...], packets, member, EARLY, rank)

    ids0 = lax.broadcasted_iota(jnp.int32, (total, total), 0)
    ids1 = lax.broadcasted_iota(jnp.int32, (total, total), 1)
    diagonal = ids0 == ids1
    eye = jnp.where(diagonal, 1.0, 0.0)
    own = jnp.sum(jnp.where(diagonal, kernel, 0.0), axis=0, keepdims=True)
    damp = jnp.sum(own, axis=1, keepdims=True) * (0.1 / width)
    scale = own + damp
    inverse = 1.0 / scale
    column = jnp.sum(jnp.where(diagonal, damp * inverse, 0.0), axis=1, keepdims=True)
    e1 = jnp.where(diagonal, 1.0 - RELAX, kernel * (inverse * -RELAX))
    mine = e1[:per_dev] + eye[:per_dev]
    e2 = mm(e1, e1)
    e4 = mm(e2, e2)
    mine = mine + mm(mine, e2)
    e8 = mm(e4, e4)
    mine = mine + mm(mine, e4)
    mine = mine + mm(mine, e8)
    squares = e8 * e8
    left = jnp.sum(squares * column)
    spread = jnp.sum(squares * column * (scale / damp))
    good = (left <= 2e-6) & (spread <= 0.005)
    s_ref[...] = eye[:per_dev] - RELAX * column[:per_dev] * mine

    @pl.when(jnp.logical_not(good))
    def _():
        e16 = mm(e8, e8)
        s_ref[...] = eye[:per_dev] - RELAX * column[:per_dev] * (mine + mm(mine, e16))
        near = (jnp.sum(e16 * e16 * column) <= 2e-6) & (spread <= 0.05)

        @pl.when(jnp.logical_not(near))
        def _():
            s_ref[...] = orthogonal_shares(width, per_dev, rank, packets, membership, v_ref)

    out_ref[...] = s_ref[...]


def chosen_of(total, per_dev, q):
    hops = (place_of(lax.axis_index("ex")) - place_of(q // per_dev) + len(RING)) % len(RING)
    slot = jnp.zeros_like(hops)
    for k, h in enumerate(HOPS):
        slot = jnp.where(hops == h, k, slot)
    place = slot * per_dev + q % per_dev
    rows = lax.broadcasted_iota(jnp.int32, (total, q.shape[1]), 0)
    return jnp.where(rows == place, 1.0, 0.0).astype(BF16)


def score_kernel(a_ref, b_ref, c_ref, d_ref, chosen_ref, out_ref):
    chosen = chosen_ref[...]
    hi, mid, low = split3((a_ref[...] + b_ref[...]) + (c_ref[...] + d_ref[...]))
    out_ref[...] = (nn(low, chosen) + nn(mid, chosen)) + nn(hi, chosen)


def vmem():
    return pl.BlockSpec(memory_space=pltpu.VMEM)


def place_of(index):
    return (index % 2) * 2 + index // 2


def shift(x, hops):
    return lax.ppermute(x, "ex", [(RING[i], RING[(i + hops) % len(RING)]) for i in range(len(RING))])


def swap(x, axis, count, k):
    return lax.ppermute(x, axis, [(i, i ^ k) for i in range(count)])


def small_device(ex_count, layer_count, layer_inputs, out_grads, proj_in, proj_out, frame_lengths, query_ids):
    frames = layer_inputs.shape[1]
    rank = proj_in.shape[2]
    per_dev = frame_lengths.shape[1]
    total = ex_count * per_dev
    hbm = pl.BlockSpec(memory_space=pltpu.HBM)
    packet = pl.pallas_call(
        project_kernel,
        out_shape=jax.ShapeDtypeStruct((2 * rank + 8, frames), F32),
        in_specs=[hbm] * 5,
        out_specs=vmem(),
        scratch_shapes=[
            pltpu.SMEM(frame_lengths.shape, jnp.int32),
            pltpu.VMEM(layer_inputs.shape[1:], BF16),
            pltpu.VMEM(out_grads.shape[1:], BF16),
            pltpu.VMEM((rank, proj_in.shape[1]), BF16),
            pltpu.VMEM((rank, proj_out.shape[1]), BF16),
            pltpu.SemaphoreType.DMA((4 + CHUNKS,)),
        ],
        compiler_params=pltpu.CompilerParams(vmem_limit_bytes=16 * 1024 * 1024),
        name="project",
    )(*[
        pltpu.with_memory_space_constraint(x, pltpu.HBM)
        for x in (frame_lengths, layer_inputs, out_grads, jnp.swapaxes(proj_in, 1, 2), jnp.swapaxes(proj_out, 1, 2))
    ])
    packets = [packet] + [shift(packet, hops) for hops in HOPS[1:]]
    lefts = jax.ShapeDtypeStruct((EARLY * frames, 3 * rank), BF16)
    early, chosen, left_o, left_i = pl.pallas_call(
        functools.partial(early_kernel, per_dev, rank),
        out_shape=(jax.ShapeDtypeStruct((total, total), F32), jax.ShapeDtypeStruct((total, query_ids.shape[0]), BF16), lefts, lefts),
        in_specs=[vmem()] * (1 + EARLY),
        out_specs=(vmem(),) * 4,
        compiler_params=pltpu.CompilerParams(vmem_limit_bytes=16 * 1024 * 1024),
        cost_estimate=pl.CostEstimate(flops=10**6, bytes_accessed=10**5, transcendentals=0),
        name="early",
    )(query_ids.reshape(1, -1), *packets[:EARLY])
    share = pl.pallas_call(
        functools.partial(solve_kernel, rank * rank, per_dev, rank),
        out_shape=jax.ShapeDtypeStruct((per_dev, total), F32),
        in_specs=[vmem()] * (ex_count + 3),
        out_specs=vmem(),
        scratch_shapes=[pltpu.VMEM((per_dev, total), F32), pltpu.VMEM((rank * rank // 128 + 1, total, 128), F32)],
        compiler_params=pltpu.CompilerParams(vmem_limit_bytes=16 * 1024 * 1024),
        name="solve",
    )(early, left_o, left_i, *packets)
    shares = [share] + [swap(share, "layer", layer_count, k) for k in range(1, layer_count)]
    scores = pl.pallas_call(
        score_kernel,
        out_shape=jax.ShapeDtypeStruct((per_dev, query_ids.shape[0]), F32),
        in_specs=[vmem()] * 5,
        out_specs=vmem(),
        compiler_params=pltpu.CompilerParams(vmem_limit_bytes=16 * 1024 * 1024),
        name="score",
    )(*shares, chosen)
    return scores.T


def large_device(layer_inputs, out_grads, proj_in, proj_out, frame_lengths, query_ids):
    frame_count = layer_inputs.shape[1]
    in_proj = jnp.dot(layer_inputs[0], proj_in[0], preferred_element_type=F32)
    out_proj = jnp.dot(out_grads[0], proj_out[0], preferred_element_type=F32)
    rank = in_proj.shape[1]
    width = rank * rank
    outer_terms = (out_proj[:, :, None] * in_proj[:, None, :]).reshape(frame_count, width)
    lengths = frame_lengths[0]
    end_frames = jnp.cumsum(lengths)
    starts = end_frames - lengths
    positions = jnp.arange(frame_count, dtype=jnp.int32)
    member = ((positions[None, :] >= starts[:, None]) & (positions[None, :] < end_frames[:, None])).astype(F32)
    features = jnp.dot(member, outer_terms, precision=lax.Precision.HIGHEST)
    all_features = lax.all_gather(features, "ex", axis=0, tiled=True)
    count = all_features.shape[0]
    kernel = lax.dot_general(
        all_features, all_features, (((1,), (1,)), ((), ())), precision=lax.Precision.HIGHEST, preferred_element_type=F32
    )
    damping = 0.1 * jnp.trace(kernel) / width
    factor = jnp.linalg.cholesky(kernel + damping * jnp.eye(count, dtype=F32))
    mine = lax.axis_index("ex") * lengths.shape[0] + jnp.arange(lengths.shape[0])
    picked = (jnp.arange(count)[:, None] == mine[None, :]).astype(F32)
    share = picked - damping * jax.scipy.linalg.cho_solve((factor, True), picked)
    summed = lax.psum(share, "layer")
    chosen = (query_ids[:, None] == jnp.arange(count, dtype=jnp.int32)[None, :]).astype(F32)
    return jnp.dot(chosen, summed, precision=lax.Precision.HIGHEST)


def solution(mesh):
    ex_count, layer_count = mesh.shape["ex"], mesh.shape["layer"]
    if ex_count == 4 and layer_count == 4:
        per_device = functools.partial(small_device, ex_count, layer_count)
    else:
        per_device = large_device
    return jax.shard_map(
        per_device,
        mesh=mesh,
        in_specs=(
            P("layer", ("groups", "ex"), None),
            P("layer", ("groups", "ex"), None),
            P("layer", None, None),
            P("layer", None, None),
            P(("groups", "ex"), None),
            P("groups"),
        ),
        out_specs=P("groups", "ex"),
        check_vma=False,
    )
```

```python
import functools

import jax
import jax.numpy as jnp
from jax import lax
from jax.experimental import pallas as pl
from jax.experimental.pallas import tpu as pltpu
from jax.sharding import PartitionSpec as P

F32 = jnp.float32
BF16 = jnp.bfloat16
CHUNKS = 4
RING = (0, 2, 1, 3)
HOPS = (0, 1, 2, 3)
EARLY = 2
RELAX = 0.92


def nt(a, b):
    return lax.dot_general(a, b, (((1,), (1,)), ((), ())), preferred_element_type=F32)


def nn(a, b):
    return lax.dot_general(a, b, (((1,), (0,)), ((), ())), preferred_element_type=F32)


def tn(a, b):
    return lax.dot_general(a, b, (((0,), (0,)), ((), ())), preferred_element_type=F32)


def split3(x):
    hi = x.astype(BF16)
    rest = x - hi.astype(F32)
    mid = rest.astype(BF16)
    low = (rest - mid.astype(F32)).astype(BF16)
    return hi, mid, low


def split2(x):
    hi = x.astype(BF16)
    return hi, (x - hi.astype(F32)).astype(BF16)


def mm(a, b):
    ah, al = split2(a)
    bh, bl = split2(b)
    return (nn(ah, bl) + nn(al, bh)) + nn(ah, bh)


def exact(a, b, dims):
    return lax.dot_general(a, b, (dims, ((), ())), precision=lax.Precision.HIGHEST, preferred_element_type=F32)


def project_kernel(lens_hbm, li_ref, og_ref, pi_ref, po_ref, out_ref, lens_ref, li_v, og_v, pi_v, po_v, sems):
    ff = og_ref.shape[2]
    step = ff // CHUNKS
    copies = [
        pltpu.make_async_copy(pi_ref.at[0], pi_v, sems.at[0]),
        pltpu.make_async_copy(li_ref.at[0], li_v, sems.at[1]),
        pltpu.make_async_copy(po_ref.at[0], po_v, sems.at[2]),
        pltpu.make_async_copy(lens_hbm, lens_ref, sems.at[3]),
    ]
    for c in range(CHUNKS):
        cols = pl.ds(c * step, step)
        copies.append(pltpu.make_async_copy(og_ref.at[0, :, cols], og_v.at[:, cols], sems.at[4 + c]))
    for copy in copies:
        copy.start()
    rank = pi_ref.shape[1]
    frames = li_ref.shape[1]
    positions = lax.broadcasted_iota(jnp.int32, (8, frames), 1)
    copies[3].wait()
    ids = jnp.zeros((8, frames), F32)
    end = lens_ref[0, 0]
    for j in range(1, lens_ref.shape[1]):
        ids = ids + jnp.where(positions >= end, 1.0, 0.0)
        end = end + lens_ref[0, j]
    out_ref[2 * rank:, :] = ids
    copies[0].wait()
    copies[1].wait()
    out_ref[rank:2 * rank, :] = nt(pi_v[...], li_v[...])
    copies[2].wait()
    total = jnp.zeros((rank, frames), F32)
    for c in range(CHUNKS):
        copies[4 + c].wait()
        total = total + nt(po_v[:, c * step:(c + 1) * step], og_v[:, c * step:(c + 1) * step])
    out_ref[:rank, :] = total


def orthogonal_shares(width, per_dev, rank, packets, member, v_ref):
    total = member.shape[0]
    blocks, lanes = v_ref.shape[0] - 1, v_ref.shape[2]
    per = lanes // rank
    in_proj = jnp.concatenate([jnp.concatenate([p[rank:2 * rank, :] for p in packets], axis=1)] * per, axis=0)
    owner = lax.broadcasted_iota(jnp.int32, in_proj.shape, 0) // rank

    def fill(g, carry):
        block = jnp.zeros((total, lanes), F32)
        for s in range(per):
            out_row = jnp.concatenate([p[pl.ds(g * per + s, 1), :] for p in packets], axis=1)
            block = block + exact(member * out_row, jnp.where(owner == s, in_proj, 0.0), ((1,), (1,)))
        v_ref[pl.ds(g, 1)] = block[None]
        return carry

    lax.fori_loop(0, blocks, fill, 0)
    features = v_ref[:blocks]
    damp = jnp.sum(features * features, keepdims=True)[0] * (0.1 / width)
    row = lax.broadcasted_iota(jnp.int32, (total, lanes), 0)
    lane = lax.broadcasted_iota(jnp.int32, (total, lanes), 1)
    v_ref[blocks] = jnp.where(row == lane, jnp.sqrt(damp), 0.0)

    def step(k, carry):
        v = v_ref[...]
        rows = lax.broadcasted_iota(jnp.int32, v.shape, 1)
        q = jnp.sum(jnp.where(rows == k, v, 0.0), axis=1, keepdims=True)
        size = jnp.sum(jnp.sum(q * q, axis=0, keepdims=True), axis=2, keepdims=True)
        q = q / jnp.sqrt(size)
        along = jnp.sum(jnp.sum(v * q, axis=0, keepdims=True), axis=2, keepdims=True)
        v_ref[...] = jnp.where(rows > k, v - along * q, jnp.where(rows == k, q, v))
        return carry

    lax.fori_loop(0, total, step, 0)
    last = v_ref[blocks]
    inverse = exact(last, last, ((0,), (0,)))
    return jnp.where(row == lane, 1.0, 0.0)[:per_dev, :total] - inverse[:per_dev, :total]


def terms(packets, lo, rank):
    hi, low = split2(jnp.concatenate([p[lo:lo + rank, :] for p in packets], axis=1))
    return jnp.concatenate([hi, hi, low], axis=0), jnp.concatenate([hi, low, hi], axis=0)


def members(packet, first, total, rank):
    row = lax.broadcasted_iota(jnp.int32, (total, packet.shape[1]), 0).astype(F32)
    return jnp.where(packet[2 * rank:2 * rank + 1, :] + float(first) == row, 1.0, 0.0)


def early_kernel(per_dev, rank, query_ref, *refs):
    packets, (out_ref, chosen_ref, left_o_ref, left_i_ref, first_ref) = refs[:-5], refs[-5:]
    total = out_ref.shape[0]
    chosen_ref[...] = chosen_of(total, per_dev, query_ref[...])
    member = jnp.concatenate([members(p, k * per_dev, total, rank) for k, p in enumerate(packets)], axis=1).astype(BF16)
    left_o, right_o = terms(packets, 0, rank)
    left_i, right_i = terms(packets, rank, rank)
    first_ref[...] = member
    left_o, left_i = left_o.T, left_i.T
    left_o_ref[...] = left_o
    left_i_ref[...] = left_i
    hi, low = split2(nn(left_o, right_o) * nn(left_i, right_i))
    hi, low = split2(nn(member, low) + nn(member, hi))
    out_ref[...] = nt(low, member) + nt(hi, member)


def extend(known, left_o, left_i, packets, member, skip, rank):
    frames = packets[0].shape[1]
    first, late = member[:, :skip * frames], member[:, skip * frames:]
    late_o, right_o = terms(packets[skip:], 0, rank)
    late_i, right_i = terms(packets[skip:], rank, rank)
    cross_hi, cross_low = split2(nn(left_o, right_o) * nn(left_i, right_i))
    own_hi, own_low = split2(tn(late_o, right_o) * tn(late_i, right_i))
    cross = nn(first, cross_low) + nn(first, cross_hi)
    hi, low = split2(cross + (nn(late, own_low) + nn(late, own_hi)))
    columns = nt(low, late) + nt(hi, late)
    hi, low = split2(cross)
    return known + (columns + (nt(late, low) + nt(late, hi)))


def solve_kernel(width, per_dev, rank, *refs):
    early_ref, left_o_ref, left_i_ref, first_ref = refs[:4]
    packets, (out_ref, v_ref) = refs[4:-2], refs[-2:]
    frames = packets[0].shape[1]
    count = len(packets)
    total = count * per_dev

    late = [members(p, k * per_dev, total, rank) for k, p in list(enumerate(packets))[EARLY:]]
    member = jnp.concatenate([first_ref[...]] + [part.astype(BF16) for part in late], axis=1)
    kernel = extend(early_ref[...], left_o_ref[...], left_i_ref[...], packets, member, EARLY, rank)

    ids0 = lax.broadcasted_iota(jnp.int32, (total, total), 0)
    ids1 = lax.broadcasted_iota(jnp.int32, (total, total), 1)
    diagonal = ids0 == ids1
    eye = jnp.where(diagonal, 1.0, 0.0)
    own = jnp.sum(jnp.where(diagonal, kernel, 0.0), axis=0, keepdims=True)
    damp = jnp.sum(own, axis=1, keepdims=True) * (0.1 / width)
    scale = own + damp
    inverse = 1.0 / scale
    column = jnp.sum(jnp.where(diagonal, damp * inverse, 0.0), axis=1, keepdims=True)
    e1 = jnp.where(diagonal, 1.0 - RELAX, kernel * (inverse * -RELAX))
    mine = e1[:per_dev] + eye[:per_dev]
    e2 = mm(e1, e1)
    e4 = mm(e2, e2)
    mine = mine + mm(mine, e2)
    e8 = mm(e4, e4)
    mine = mine + mm(mine, e4)
    mine = mine + mm(mine, e8)
    squares = e8 * e8
    left = jnp.sum(squares * column)
    spread = jnp.sum(squares * column * (scale / damp))
    good = (left <= 2e-6) & (spread <= 0.005)
    out_ref[...] = eye[:per_dev] - RELAX * column[:per_dev] * mine

    @pl.when(jnp.logical_not(good))
    def _():
        e16 = mm(e8, e8)
        out_ref[...] = eye[:per_dev] - RELAX * column[:per_dev] * (mine + mm(mine, e16))
        near = (jnp.sum(e16 * e16 * column) <= 2e-6) & (spread <= 0.05)

        @pl.when(jnp.logical_not(near))
        def _():
            out_ref[...] = orthogonal_shares(width, per_dev, rank, packets, member.astype(F32), v_ref)


def chosen_of(total, per_dev, q):
    hops = (place_of(lax.axis_index("ex")) - place_of(q // per_dev) + len(RING)) % len(RING)
    slot = jnp.zeros_like(hops)
    for k, h in enumerate(HOPS):
        slot = jnp.where(hops == h, k, slot)
    place = slot * per_dev + q % per_dev
    rows = lax.broadcasted_iota(jnp.int32, (total, q.shape[1]), 0)
    return jnp.where(rows == place, 1.0, 0.0).astype(BF16)


def score_kernel(a_ref, b_ref, c_ref, d_ref, chosen_ref, out_ref):
    chosen = chosen_ref[...]
    hi, mid, low = split3((a_ref[...] + b_ref[...]) + (c_ref[...] + d_ref[...]))
    out_ref[...] = (nn(low, chosen) + nn(mid, chosen)) + nn(hi, chosen)


def vmem():
    return pl.BlockSpec(memory_space=pltpu.VMEM)


def place_of(index):
    return (index % 2) * 2 + index // 2


def shift(x, hops):
    return lax.ppermute(x, "ex", [(RING[i], RING[(i + hops) % len(RING)]) for i in range(len(RING))])


def swap(x, axis, count, k):
    return lax.ppermute(x, axis, [(i, i ^ k) for i in range(count)])


def small_device(ex_count, layer_count, layer_inputs, out_grads, proj_in, proj_out, frame_lengths, query_ids):
    frames = layer_inputs.shape[1]
    rank = proj_in.shape[2]
    per_dev = frame_lengths.shape[1]
    total = ex_count * per_dev
    hbm = pl.BlockSpec(memory_space=pltpu.HBM)
    packet = pl.pallas_call(
        project_kernel,
        out_shape=jax.ShapeDtypeStruct((2 * rank + 8, frames), F32),
        in_specs=[hbm] * 5,
        out_specs=vmem(),
        scratch_shapes=[
            pltpu.SMEM(frame_lengths.shape, jnp.int32),
            pltpu.VMEM(layer_inputs.shape[1:], BF16),
            pltpu.VMEM(out_grads.shape[1:], BF16),
            pltpu.VMEM((rank, proj_in.shape[1]), BF16),
            pltpu.VMEM((rank, proj_out.shape[1]), BF16),
            pltpu.SemaphoreType.DMA((4 + CHUNKS,)),
        ],
        compiler_params=pltpu.CompilerParams(vmem_limit_bytes=16 * 1024 * 1024),
        name="project",
    )(*[
        pltpu.with_memory_space_constraint(x, pltpu.HBM)
        for x in (frame_lengths, layer_inputs, out_grads, jnp.swapaxes(proj_in, 1, 2), jnp.swapaxes(proj_out, 1, 2))
    ])
    packets = [packet] + [shift(packet, hops) for hops in HOPS[1:]]
    lefts = jax.ShapeDtypeStruct((EARLY * frames, 3 * rank), BF16)
    early, chosen, left_o, left_i, first = pl.pallas_call(
        functools.partial(early_kernel, per_dev, rank),
        out_shape=(jax.ShapeDtypeStruct((total, total), F32), jax.ShapeDtypeStruct((total, query_ids.shape[0]), BF16), lefts, lefts, jax.ShapeDtypeStruct((total, EARLY * frames), BF16)),
        in_specs=[vmem()] * (1 + EARLY),
        out_specs=(vmem(),) * 5,
        compiler_params=pltpu.CompilerParams(vmem_limit_bytes=16 * 1024 * 1024),
        cost_estimate=pl.CostEstimate(flops=10**6, bytes_accessed=10**5, transcendentals=0),
        name="early",
    )(query_ids.reshape(1, -1), *packets[:EARLY])
    share = pl.pallas_call(
        functools.partial(solve_kernel, rank * rank, per_dev, rank),
        out_shape=jax.ShapeDtypeStruct((per_dev, total), F32),
        in_specs=[vmem()] * (ex_count + 4),
        out_specs=vmem(),
        scratch_shapes=[pltpu.VMEM((rank * rank // 128 + 1, total, 128), F32)],
        compiler_params=pltpu.CompilerParams(vmem_limit_bytes=16 * 1024 * 1024),
        name="solve",
    )(early, left_o, left_i, first, *packets)
    shares = [share] + [swap(share, "layer", layer_count, k) for k in range(1, layer_count)]
    scores = pl.pallas_call(
        score_kernel,
        out_shape=jax.ShapeDtypeStruct((per_dev, query_ids.shape[0]), F32),
        in_specs=[vmem()] * 5,
        out_specs=vmem(),
        compiler_params=pltpu.CompilerParams(vmem_limit_bytes=16 * 1024 * 1024),
        name="score",
    )(*shares, chosen)
    return scores.T


def large_device(layer_inputs, out_grads, proj_in, proj_out, frame_lengths, query_ids):
    frame_count = layer_inputs.shape[1]
    in_proj = jnp.dot(layer_inputs[0], proj_in[0], preferred_element_type=F32)
    out_proj = jnp.dot(out_grads[0], proj_out[0], preferred_element_type=F32)
    rank = in_proj.shape[1]
    width = rank * rank
    outer_terms = (out_proj[:, :, None] * in_proj[:, None, :]).reshape(frame_count, width)
    lengths = frame_lengths[0]
    end_frames = jnp.cumsum(lengths)
    starts = end_frames - lengths
    positions = jnp.arange(frame_count, dtype=jnp.int32)
    member = ((positions[None, :] >= starts[:, None]) & (positions[None, :] < end_frames[:, None])).astype(F32)
    features = jnp.dot(member, outer_terms, precision=lax.Precision.HIGHEST)
    all_features = lax.all_gather(features, "ex", axis=0, tiled=True)
    count = all_features.shape[0]
    kernel = lax.dot_general(
        all_features, all_features, (((1,), (1,)), ((), ())), precision=lax.Precision.HIGHEST, preferred_element_type=F32
    )
    damping = 0.1 * jnp.trace(kernel) / width
    factor = jnp.linalg.cholesky(kernel + damping * jnp.eye(count, dtype=F32))
    mine = lax.axis_index("ex") * lengths.shape[0] + jnp.arange(lengths.shape[0])
    picked = (jnp.arange(count)[:, None] == mine[None, :]).astype(F32)
    share = picked - damping * jax.scipy.linalg.cho_solve((factor, True), picked)
    summed = lax.psum(share, "layer")
    chosen = (query_ids[:, None] == jnp.arange(count, dtype=jnp.int32)[None, :]).astype(F32)
    return jnp.dot(chosen, summed, precision=lax.Precision.HIGHEST)


def solution(mesh):
    ex_count, layer_count = mesh.shape["ex"], mesh.shape["layer"]
    if ex_count == 4 and layer_count == 4:
        per_device = functools.partial(small_device, ex_count, layer_count)
    else:
        per_device = large_device
    return jax.shard_map(
        per_device,
        mesh=mesh,
        in_specs=(
            P("layer", ("groups", "ex"), None),
            P("layer", ("groups", "ex"), None),
            P("layer", None, None),
            P("layer", None, None),
            P(("groups", "ex"), None),
            P("groups"),
        ),
        out_specs=P("groups", "ex"),
        check_vma=False,
    )
```

```python
import functools

import jax
import jax.numpy as jnp
from jax import lax
from jax.experimental import pallas as pl
from jax.experimental.pallas import tpu as pltpu
from jax.sharding import PartitionSpec as P

F32 = jnp.float32
BF16 = jnp.bfloat16
CUTS = (0, 1, 3, 5)
RING = (0, 2, 1, 3)
HOPS = (0, 1, 2, 3)
EARLY = 2
RELAX = 0.92


def nt(a, b):
    return lax.dot_general(a, b, (((1,), (1,)), ((), ())), preferred_element_type=F32)


def nn(a, b):
    return lax.dot_general(a, b, (((1,), (0,)), ((), ())), preferred_element_type=F32)


def tn(a, b):
    return lax.dot_general(a, b, (((0,), (0,)), ((), ())), preferred_element_type=F32)


def split3(x):
    hi = x.astype(BF16)
    rest = x - hi.astype(F32)
    mid = rest.astype(BF16)
    low = (rest - mid.astype(F32)).astype(BF16)
    return hi, mid, low


def split2(x):
    hi = x.astype(BF16)
    return hi, (x - hi.astype(F32)).astype(BF16)


def mm(a, b):
    ah, al = split2(a)
    bh, bl = split2(b)
    return (nn(ah, bl) + nn(al, bh)) + nn(ah, bh)


def exact(a, b, dims):
    return lax.dot_general(a, b, (dims, ((), ())), precision=lax.Precision.HIGHEST, preferred_element_type=F32)


def project_kernel(lens_hbm, li_ref, og_ref, pi_ref, po_ref, out_ref, lens_ref, li_v, og_v, pi_v, po_v, sems):
    ff = og_ref.shape[2]
    cuts = [ff * cut // CUTS[-1] for cut in CUTS]
    chunks = [slice(lo, hi) for lo, hi in zip(cuts, cuts[1:])]
    copies = [
        pltpu.make_async_copy(pi_ref.at[0], pi_v, sems.at[0]),
        pltpu.make_async_copy(li_ref.at[0], li_v, sems.at[1]),
        pltpu.make_async_copy(po_ref.at[0], po_v, sems.at[2]),
        pltpu.make_async_copy(lens_hbm, lens_ref, sems.at[3]),
    ]
    for c, cols in enumerate(chunks):
        copies.append(pltpu.make_async_copy(og_ref.at[0, :, cols], og_v.at[:, cols], sems.at[4 + c]))
    for copy in copies:
        copy.start()
    rank = pi_ref.shape[1]
    frames = li_ref.shape[1]
    positions = lax.broadcasted_iota(jnp.int32, (8, frames), 1)
    copies[3].wait()
    ids = jnp.zeros((8, frames), F32)
    end = lens_ref[0, 0]
    for j in range(1, lens_ref.shape[1]):
        ids = ids + jnp.where(positions >= end, 1.0, 0.0)
        end = end + lens_ref[0, j]
    out_ref[2 * rank:, :] = ids
    copies[0].wait()
    copies[1].wait()
    out_ref[rank:2 * rank, :] = nt(pi_v[...], li_v[...])
    copies[2].wait()
    total = jnp.zeros((rank, frames), F32)
    for c, cols in enumerate(chunks):
        copies[4 + c].wait()
        total = total + nt(po_v[:, cols], og_v[:, cols])
    out_ref[:rank, :] = total


def orthogonal_shares(width, per_dev, rank, packets, member, v_ref):
    total = member.shape[0]
    blocks, lanes = v_ref.shape[0] - 1, v_ref.shape[2]
    per = lanes // rank
    in_proj = jnp.concatenate([jnp.concatenate([p[rank:2 * rank, :] for p in packets], axis=1)] * per, axis=0)
    owner = lax.broadcasted_iota(jnp.int32, in_proj.shape, 0) // rank

    def fill(g, carry):
        block = jnp.zeros((total, lanes), F32)
        for s in range(per):
            out_row = jnp.concatenate([p[pl.ds(g * per + s, 1), :] for p in packets], axis=1)
            block = block + exact(member * out_row, jnp.where(owner == s, in_proj, 0.0), ((1,), (1,)))
        v_ref[pl.ds(g, 1)] = block[None]
        return carry

    lax.fori_loop(0, blocks, fill, 0)
    features = v_ref[:blocks]
    damp = jnp.sum(features * features, keepdims=True)[0] * (0.1 / width)
    row = lax.broadcasted_iota(jnp.int32, (total, lanes), 0)
    lane = lax.broadcasted_iota(jnp.int32, (total, lanes), 1)
    v_ref[blocks] = jnp.where(row == lane, jnp.sqrt(damp), 0.0)

    def step(k, carry):
        v = v_ref[...]
        rows = lax.broadcasted_iota(jnp.int32, v.shape, 1)
        q = jnp.sum(jnp.where(rows == k, v, 0.0), axis=1, keepdims=True)
        size = jnp.sum(jnp.sum(q * q, axis=0, keepdims=True), axis=2, keepdims=True)
        q = q / jnp.sqrt(size)
        along = jnp.sum(jnp.sum(v * q, axis=0, keepdims=True), axis=2, keepdims=True)
        v_ref[...] = jnp.where(rows > k, v - along * q, jnp.where(rows == k, q, v))
        return carry

    lax.fori_loop(0, total, step, 0)
    last = v_ref[blocks]
    inverse = exact(last, last, ((0,), (0,)))
    return jnp.where(row == lane, 1.0, 0.0)[:per_dev, :total] - inverse[:per_dev, :total]


def terms(packets, lo, rank):
    hi, low = split2(jnp.concatenate([p[lo:lo + rank, :] for p in packets], axis=1))
    return jnp.concatenate([hi, hi, low], axis=0), jnp.concatenate([hi, low, hi], axis=0)


def members(packet, first, total, rank):
    row = lax.broadcasted_iota(jnp.int32, (total, packet.shape[1]), 0).astype(F32)
    return jnp.where(packet[2 * rank:2 * rank + 1, :] + float(first) == row, 1.0, 0.0)


def early_kernel(per_dev, rank, query_ref, *refs):
    packets, (out_ref, chosen_ref, left_o_ref, left_i_ref, first_ref) = refs[:-5], refs[-5:]
    total = out_ref.shape[0]
    chosen_ref[...] = chosen_of(total, per_dev, query_ref[...])
    member = jnp.concatenate([members(p, k * per_dev, total, rank) for k, p in enumerate(packets)], axis=1).astype(BF16)
    left_o, right_o = terms(packets, 0, rank)
    left_i, right_i = terms(packets, rank, rank)
    first_ref[...] = member
    left_o, left_i = left_o.T, left_i.T
    left_o_ref[...] = left_o
    left_i_ref[...] = left_i
    hi, low = split2(nn(left_o, right_o) * nn(left_i, right_i))
    hi, low = split2(nn(member, low) + nn(member, hi))
    out_ref[...] = nt(low, member) + nt(hi, member)


def extend(known, left_o, left_i, packets, member, skip, rank):
    frames = packets[0].shape[1]
    first, late = member[:, :skip * frames], member[:, skip * frames:]
    late_o, right_o = terms(packets[skip:], 0, rank)
    late_i, right_i = terms(packets[skip:], rank, rank)
    cross_hi, cross_low = split2(nn(left_o, right_o) * nn(left_i, right_i))
    own_hi, own_low = split2(tn(late_o, right_o) * tn(late_i, right_i))
    cross = nn(first, cross_low) + nn(first, cross_hi)
    hi, low = split2(cross + (nn(late, own_low) + nn(late, own_hi)))
    columns = nt(low, late) + nt(hi, late)
    hi, low = split2(cross)
    return known + (columns + (nt(late, low) + nt(late, hi)))


def solve_kernel(width, per_dev, rank, *refs):
    early_ref, left_o_ref, left_i_ref, first_ref = refs[:4]
    packets, (out_ref, v_ref) = refs[4:-2], refs[-2:]
    frames = packets[0].shape[1]
    count = len(packets)
    total = count * per_dev

    late = [members(p, k * per_dev, total, rank) for k, p in list(enumerate(packets))[EARLY:]]
    member = jnp.concatenate([first_ref[...]] + [part.astype(BF16) for part in late], axis=1)
    kernel = extend(early_ref[...], left_o_ref[...], left_i_ref[...], packets, member, EARLY, rank)

    ids0 = lax.broadcasted_iota(jnp.int32, (total, total), 0)
    ids1 = lax.broadcasted_iota(jnp.int32, (total, total), 1)
    diagonal = ids0 == ids1
    eye = jnp.where(diagonal, 1.0, 0.0)
    own = jnp.sum(jnp.where(diagonal, kernel, 0.0), axis=0, keepdims=True)
    damp = jnp.sum(own, axis=1, keepdims=True) * (0.1 / width)
    scale = own + damp
    inverse = 1.0 / scale
    column = jnp.sum(jnp.where(diagonal, damp * inverse, 0.0), axis=1, keepdims=True)
    e1 = jnp.where(diagonal, 1.0 - RELAX, kernel * (inverse * -RELAX))
    mine = e1[:per_dev] + eye[:per_dev]
    e2 = mm(e1, e1)
    e4 = mm(e2, e2)
    mine = mine + mm(mine, e2)
    e8 = mm(e4, e4)
    mine = mine + mm(mine, e4)
    mine = mine + mm(mine, e8)
    squares = e8 * e8
    left = jnp.sum(squares * column)
    spread = jnp.sum(squares * column * (scale / damp))
    good = (left <= 2e-6) & (spread <= 0.005)
    out_ref[...] = eye[:per_dev] - RELAX * column[:per_dev] * mine

    @pl.when(jnp.logical_not(good))
    def _():
        e16 = mm(e8, e8)
        out_ref[...] = eye[:per_dev] - RELAX * column[:per_dev] * (mine + mm(mine, e16))
        near = (jnp.sum(e16 * e16 * column) <= 2e-6) & (spread <= 0.05)

        @pl.when(jnp.logical_not(near))
        def _():
            out_ref[...] = orthogonal_shares(width, per_dev, rank, packets, member.astype(F32), v_ref)


def chosen_of(total, per_dev, q):
    hops = (place_of(lax.axis_index("ex")) - place_of(q // per_dev) + len(RING)) % len(RING)
    slot = jnp.zeros_like(hops)
    for k, h in enumerate(HOPS):
        slot = jnp.where(hops == h, k, slot)
    place = slot * per_dev + q % per_dev
    rows = lax.broadcasted_iota(jnp.int32, (total, q.shape[1]), 0)
    return jnp.where(rows == place, 1.0, 0.0).astype(BF16)


def score_kernel(a_ref, b_ref, c_ref, d_ref, chosen_ref, out_ref):
    chosen = chosen_ref[...]
    hi, mid, low = split3((a_ref[...] + b_ref[...]) + (c_ref[...] + d_ref[...]))
    out_ref[...] = (nn(low, chosen) + nn(mid, chosen)) + nn(hi, chosen)


def vmem():
    return pl.BlockSpec(memory_space=pltpu.VMEM)


def place_of(index):
    return (index % 2) * 2 + index // 2


def shift(x, hops):
    return lax.ppermute(x, "ex", [(RING[i], RING[(i + hops) % len(RING)]) for i in range(len(RING))])


def swap(x, axis, count, k):
    return lax.ppermute(x, axis, [(i, i ^ k) for i in range(count)])


def small_device(ex_count, layer_count, layer_inputs, out_grads, proj_in, proj_out, frame_lengths, query_ids):
    frames = layer_inputs.shape[1]
    rank = proj_in.shape[2]
    per_dev = frame_lengths.shape[1]
    total = ex_count * per_dev
    hbm = pl.BlockSpec(memory_space=pltpu.HBM)
    packet = pl.pallas_call(
        project_kernel,
        out_shape=jax.ShapeDtypeStruct((2 * rank + 8, frames), F32),
        in_specs=[hbm] * 5,
        out_specs=vmem(),
        scratch_shapes=[
            pltpu.SMEM(frame_lengths.shape, jnp.int32),
            pltpu.VMEM(layer_inputs.shape[1:], BF16),
            pltpu.VMEM(out_grads.shape[1:], BF16),
            pltpu.VMEM((rank, proj_in.shape[1]), BF16),
            pltpu.VMEM((rank, proj_out.shape[1]), BF16),
            pltpu.SemaphoreType.DMA((3 + len(CUTS),)),
        ],
        compiler_params=pltpu.CompilerParams(vmem_limit_bytes=16 * 1024 * 1024),
        name="project",
    )(*[
        pltpu.with_memory_space_constraint(x, pltpu.HBM)
        for x in (frame_lengths, layer_inputs, out_grads, jnp.swapaxes(proj_in, 1, 2), jnp.swapaxes(proj_out, 1, 2))
    ])
    packets = [packet] + [shift(packet, hops) for hops in HOPS[1:]]
    lefts = jax.ShapeDtypeStruct((EARLY * frames, 3 * rank), BF16)
    early, chosen, left_o, left_i, first = pl.pallas_call(
        functools.partial(early_kernel, per_dev, rank),
        out_shape=(jax.ShapeDtypeStruct((total, total), F32), jax.ShapeDtypeStruct((total, query_ids.shape[0]), BF16), lefts, lefts, jax.ShapeDtypeStruct((total, EARLY * frames), BF16)),
        in_specs=[vmem()] * (1 + EARLY),
        out_specs=(vmem(),) * 5,
        compiler_params=pltpu.CompilerParams(vmem_limit_bytes=16 * 1024 * 1024),
        cost_estimate=pl.CostEstimate(flops=10**6, bytes_accessed=10**5, transcendentals=0),
        name="early",
    )(query_ids.reshape(1, -1), *packets[:EARLY])
    share = pl.pallas_call(
        functools.partial(solve_kernel, rank * rank, per_dev, rank),
        out_shape=jax.ShapeDtypeStruct((per_dev, total), F32),
        in_specs=[vmem()] * (ex_count + 4),
        out_specs=vmem(),
        scratch_shapes=[pltpu.VMEM((rank * rank // 128 + 1, total, 128), F32)],
        compiler_params=pltpu.CompilerParams(vmem_limit_bytes=16 * 1024 * 1024),
        name="solve",
    )(early, left_o, left_i, first, *packets)
    shares = [share] + [swap(share, "layer", layer_count, k) for k in range(1, layer_count)]
    scores = pl.pallas_call(
        score_kernel,
        out_shape=jax.ShapeDtypeStruct((per_dev, query_ids.shape[0]), F32),
        in_specs=[vmem()] * 5,
        out_specs=vmem(),
        compiler_params=pltpu.CompilerParams(vmem_limit_bytes=16 * 1024 * 1024),
        name="score",
    )(*shares, chosen)
    return scores.T


def large_device(layer_inputs, out_grads, proj_in, proj_out, frame_lengths, query_ids):
    frame_count = layer_inputs.shape[1]
    in_proj = jnp.dot(layer_inputs[0], proj_in[0], preferred_element_type=F32)
    out_proj = jnp.dot(out_grads[0], proj_out[0], preferred_element_type=F32)
    rank = in_proj.shape[1]
    width = rank * rank
    outer_terms = (out_proj[:, :, None] * in_proj[:, None, :]).reshape(frame_count, width)
    lengths = frame_lengths[0]
    end_frames = jnp.cumsum(lengths)
    starts = end_frames - lengths
    positions = jnp.arange(frame_count, dtype=jnp.int32)
    member = ((positions[None, :] >= starts[:, None]) & (positions[None, :] < end_frames[:, None])).astype(F32)
    features = jnp.dot(member, outer_terms, precision=lax.Precision.HIGHEST)
    all_features = lax.all_gather(features, "ex", axis=0, tiled=True)
    count = all_features.shape[0]
    kernel = lax.dot_general(
        all_features, all_features, (((1,), (1,)), ((), ())), precision=lax.Precision.HIGHEST, preferred_element_type=F32
    )
    damping = 0.1 * jnp.trace(kernel) / width
    factor = jnp.linalg.cholesky(kernel + damping * jnp.eye(count, dtype=F32))
    mine = lax.axis_index("ex") * lengths.shape[0] + jnp.arange(lengths.shape[0])
    picked = (jnp.arange(count)[:, None] == mine[None, :]).astype(F32)
    share = picked - damping * jax.scipy.linalg.cho_solve((factor, True), picked)
    summed = lax.psum(share, "layer")
    chosen = (query_ids[:, None] == jnp.arange(count, dtype=jnp.int32)[None, :]).astype(F32)
    return jnp.dot(chosen, summed, precision=lax.Precision.HIGHEST)


def solution(mesh):
    ex_count, layer_count = mesh.shape["ex"], mesh.shape["layer"]
    if ex_count == 4 and layer_count == 4:
        per_device = functools.partial(small_device, ex_count, layer_count)
    else:
        per_device = large_device
    return jax.shard_map(
        per_device,
        mesh=mesh,
        in_specs=(
            P("layer", ("groups", "ex"), None),
            P("layer", ("groups", "ex"), None),
            P("layer", None, None),
            P("layer", None, None),
            P(("groups", "ex"), None),
            P("groups"),
        ),
        out_specs=P("groups", "ex"),
        check_vma=False,
    )
```
